32 devices in a mesh: section: 2 (over x), fsdp: 16 (over z, y, core).
Axes of the slice: x: 2, y: 2, z: 4, core: 2. Of those that a mesh axis runs over, the one named last changes fastest.
Arguments:
- images: bfloat16 [4, 64, 196, 512], P(None, 'fsdp'), may hold values from -6 to 6
- live_counts: int32 [4, 16], P(None, 'fsdp'), may hold values from 1 to 4, as said below
- norm_gains: bfloat16 [2, 2, 512], P('section', None, 'fsdp'), may hold values from 0.099609375 to 1.8984375
- vectors: bfloat16 [2, 6, 512], P('section', None, 'fsdp'), may hold values from -3 to 3
- qkv_weight: bfloat16 [2, 512, 1536], P('section', 'fsdp'), may hold values from -0.25 to 0.25
- proj_weight: bfloat16 [2, 512, 512], P('section', 'fsdp'), may hold values from -0.5 to 0.5
- hidden_weight: bfloat16 [2, 512, 2048], P('section', 'fsdp'), may hold values from -0.25 to 0.25
- hidden_bias: bfloat16 [2, 2048], P('section', 'fsdp'), may hold values from -3 to 3
- out_weight: bfloat16 [2, 2048, 512], P('section', 'fsdp'), may hold values from -0.125 to 0.125
- bias_table: float32 [2, 169, 16], P('section'), may hold values from -4 to 4
- out_grad: bfloat16 [4, 64, 196, 512], P(None, 'fsdp'), may hold values from -6 to 6
Outputs:
- layer_outputs: bfloat16 [2, 4, 64, 196, 512], P('section', None, 'fsdp')
- input_grads: float32 [2, 4, 64, 196, 512], P('section', None, 'fsdp')
- grad_norm_gains: float32 [2, 2, 512], P('section', None, 'fsdp')
- grad_vectors: float32 [2, 6, 512], P('section', None, 'fsdp')
- grad_qkv: float32 [2, 512, 1536], P('section', 'fsdp')
- grad_proj: float32 [2, 512, 512], P('section', 'fsdp')
- grad_hidden_weight: float32 [2, 512, 2048], P('section', 'fsdp')
- grad_hidden_bias: float32 [2, 2048], P('section', 'fsdp')
- grad_out_weight: float32 [2, 2048, 512], P('section', 'fsdp')
- grad_bias_table: float32 [2, 169, 16], P('section')
The draws below stay inside these ranges and needn't reach their ends.
Inputs may be any that keep to these rules, and one draw needn't show every extreme that they name: In each micro-batch the live images of an index of fsdp are the first live_counts of its 4 slots; some index has all 4 live and some has one.
All inputs are finite; a program needn't handle non-finite values.
Results may differ from the reference program's by a relative error of at most 0.019.
Values may be sent and summed in bfloat16 or wider, within the bound.
No kernel may reach another device: no remote copies, remote signals or barrier semaphores. Data moves between devices by JAX's collectives and lax.ppermute only.
A program may use at most 384 MiB of HBM per device.

```python
import jax
import jax.numpy as jnp
from jax import lax

D = 512
HEADS = 16
FF = 2048
WIN = 7
GRID = 14
SHIFT = 3
MICRO = 4
SLOTS = 4
TOK_IMG = 196
TABLE = 169
SECTIONS = 2
SHARDS = 16
IMAGES = 64


def draw_live_counts(key, part):
    key = jax.random.fold_in(key, 11)
    first_key, second_key, third_key = jax.random.split(key, 3)
    counts = jax.random.randint(first_key, (MICRO, SHARDS), 1, SLOTS + 1)
    fullest = jax.random.randint(second_key, (), 0, SHARDS)
    emptiest = jax.random.randint(third_key, (), 0, SHARDS)
    counts = counts.at[0, fullest].set(SLOTS)
    counts = counts.at[1, emptiest].set(1)
    return counts.astype(jnp.int32)


def steps_of(key, dims, cuts, low, top_value):
    def one(axis_at, blocks):
        heights = jax.random.uniform(jax.random.fold_in(jax.random.fold_in(key, 6), axis_at), (blocks,), jnp.float32, low / len(cuts), top_value / len(cuts))
        return jnp.repeat(jnp.exp(heights), dims[axis_at] // blocks).reshape((-1,) + (1,) * (len(dims) - axis_at - 1))

    gain = one(*cuts[0])
    for cut in cuts[1:]:
        gain = gain * one(*cut)
    return gain


def noise(stream_key, extent, deviation, bound, shards=(), dtype=jnp.bfloat16):
    array = deviation * jax.random.normal(stream_key, extent, jnp.float32)
    if shards:
        array = array * steps_of(stream_key, extent, shards, -0.22, 0.18)
    return jnp.clip(array, -bound, bound).astype(dtype)


def setup_inputs(seed: int = 0) -> dict:
    seeds = jax.random.split(jax.random.key(seed), 12)
    images = noise(seeds[0], (MICRO, IMAGES, TOK_IMG, D), 1.0, 6.0, ((1, 16),))
    live_counts = draw_live_counts(jax.random.fold_in(seeds[11], 71), 0)
    norm_gains = jnp.clip(1.0 + 0.18 * jax.random.normal(seeds[2], (SECTIONS, 2, D), jnp.float32), 0.099609375, 1.8984375).astype(jnp.bfloat16)
    vectors = noise(seeds[3], (SECTIONS, 6, D), 0.5, 3.0, ((0, 2), (2, 16)))
    qkv_weight = noise(seeds[4], (SECTIONS, D, 3 * D), D ** -0.5, 0.25, ((0, 2), (1, 16)))
    proj_weight = noise(seeds[5], (SECTIONS, D, D), (D // 4) ** -0.5, 0.5, ((0, 2), (1, 16)))
    hidden_weight = noise(seeds[6], (SECTIONS, D, FF), D ** -0.5, 0.25, ((0, 2), (1, 16)))
    hidden_bias = noise(seeds[7], (SECTIONS, FF), 0.5, 3.0, ((0, 2), (1, 16)))
    out_weight = noise(seeds[8], (SECTIONS, FF, D), FF ** -0.5, 0.125, ((0, 2), (1, 16)))
    bias_table = noise(seeds[9], (SECTIONS, TABLE, HEADS), 1.0, 4.0, ((0, 2),), jnp.float32)
    out_grad = noise(seeds[10], (MICRO, IMAGES, TOK_IMG, D), 1.0, 6.0, ((1, 16),))
    return {"images": images, "live_counts": live_counts, "norm_gains": norm_gains, "vectors": vectors, "qkv_weight": qkv_weight, "proj_weight": proj_weight, "hidden_weight": hidden_weight, "hidden_bias": hidden_bias, "out_weight": out_weight, "bias_table": bias_table, "out_grad": out_grad}


@jax.custom_vjp
def low(v):
    return lax.optimization_barrier(v.astype(jnp.bfloat16)).astype(jnp.float32)

@jax.custom_vjp
def low_back(v):
    return v

def low_keep(v):
    return (low(v), None)

def low_pass(kept, grad):
    return (grad,)

def back_keep(v):
    return (v, None)

def back_low(kept, grad):
    return (low(grad),)
low.defvjp(low_keep, low_pass)
low_back.defvjp(back_keep, back_low)
eps = 1e-05
highest = lax.Precision.HIGHEST

def normalize(values):
    center = values - lax.optimization_barrier(jnp.mean(values, axis=-1, keepdims=True))
    return center * lax.rsqrt(lax.optimization_barrier(jnp.mean(center * center, axis=-1, keepdims=True)) + eps)

def to_windows(values, shifted):
    features = values.shape[-1]
    grid_cells = values.reshape(-1, GRID, GRID, features)
    if shifted:
        grid_cells = jnp.roll(grid_cells, (-SHIFT, -SHIFT), (1, 2))
    side_count = GRID // WIN
    window_parts = grid_cells.reshape(-1, side_count, WIN, side_count, WIN, features)
    return window_parts.transpose(0, 1, 3, 2, 4, 5).reshape(-1, WIN * WIN, features)

def from_windows(blocks, shifted):
    features = blocks.shape[-1]
    side_count = GRID // WIN
    window_parts = blocks.reshape(-1, side_count, side_count, WIN, WIN, features).transpose(0, 1, 3, 2, 4, 5)
    grid_cells = window_parts.reshape(-1, GRID, GRID, features)
    if shifted:
        grid_cells = jnp.roll(grid_cells, (SHIFT, SHIFT), (1, 2))
    return grid_cells.reshape(-1, GRID * GRID, features)

def position_table():
    places = jnp.arange(WIN * WIN)
    row_index = places // WIN
    columns = places % WIN
    offsets = (row_index[:, None] - row_index[None, :] + WIN - 1) * (2 * WIN - 1) + columns[:, None] - columns[None, :] + WIN - 1
    return offsets.astype(jnp.int32)

def region_mask():
    line_index = jnp.arange(GRID)
    band_index = (line_index >= GRID - WIN).astype(jnp.int32) + (line_index >= GRID - SHIFT).astype(jnp.int32)
    region = band_index[:, None] * 3 + band_index[None, :]
    side_count = GRID // WIN
    region = region.reshape(side_count, WIN, side_count, WIN).transpose(0, 2, 1, 3).reshape(-1, WIN * WIN)
    return jnp.where(region[:, :, None] != region[:, None, :], -100.0, 0.0).astype(jnp.float32)

def layer_group(field_vals, live_mask, gain_rows, vector_rows, qkv_mat, proj_mat, expand_mat, expand_bias, contract_mat, table, shifted):
    features = field_vals.shape[-1]
    head_count = table.shape[-1]
    head_size = features // head_count
    first_norm = low(normalize(field_vals) * gain_rows[0] + vector_rows[0])
    blocks = to_windows(first_norm, shifted).reshape(-1, features)
    qkv_bias = jnp.concatenate([vector_rows[1], jnp.zeros_like(vector_rows[1]), vector_rows[2]])
    projected = low_back(low(jnp.dot(blocks, qkv_mat, precision=highest) + qkv_bias))
    window_count = projected.shape[0] // (WIN * WIN)
    pieces = projected.reshape(window_count, WIN * WIN, 3, head_count, head_size)
    queries = pieces[:, :, 0]
    key_rows = pieces[:, :, 1]
    values_in = pieces[:, :, 2]
    position_bias = jnp.transpose(table[position_table()], (2, 0, 1))
    if shifted:
        region_bias = region_mask()
    else:
        region_bias = jnp.zeros(((GRID // WIN) ** 2, WIN * WIN, WIN * WIN), jnp.float32)
    scores = jnp.einsum('wihc,wjhc->whij', queries, key_rows, precision=highest) * head_size ** (-0.5)
    scores = scores.reshape(-1, (GRID // WIN) ** 2, head_count, WIN * WIN, WIN * WIN) + position_bias + region_bias[:, None]
    scores = low_back(scores.reshape(window_count, head_count, WIN * WIN, WIN * WIN))
    probs_low = low(jax.nn.softmax(scores, axis=-1))
    mixed_out = low_back(low(jnp.einsum('whij,wjhc->wihc', probs_low, values_in, precision=highest))).reshape(-1, features)
    attended = low_back(jnp.dot(mixed_out, proj_mat, precision=highest) + vector_rows[3])
    residual = field_vals + from_windows(attended.reshape(window_count, WIN * WIN, features), shifted)
    second_norm = low(normalize(residual) * gain_rows[1] + vector_rows[4])
    hidden = low_back(jnp.dot(second_norm.reshape(-1, features), expand_mat, precision=highest) + expand_bias)
    active = low(jax.nn.gelu(hidden, approximate=False))
    branch = low_back(jnp.dot(active, contract_mat, precision=highest) + vector_rows[5])
    return (residual + branch.reshape(residual.shape)) * live_mask[:, None, None]

def run_layer(field_vals, live_mask, params, shifted):
    group_size = 16
    shape_all = field_vals.shape
    grouped = field_vals.reshape(-1, group_size, shape_all[-2], shape_all[-1])
    marks = live_mask.reshape(-1, group_size)

    def one_group(pair):
        return layer_group(pair[0], pair[1], *params, shifted)
    return lax.map(jax.checkpoint(one_group), (grouped, marks)).reshape(shape_all)

def reference(images, live_counts, norm_gains, vectors, qkv_weight, proj_weight, hidden_weight, hidden_bias, out_weight, bias_table, out_grad):
    owner = (jnp.arange(IMAGES) // SLOTS).astype(jnp.int32)
    slot_index = jnp.arange(IMAGES) % SLOTS
    live_mask = (slot_index[None, :] < live_counts[:, owner]).astype(jnp.float32).reshape(-1)
    weights = tuple((member.astype(jnp.float32) for member in (norm_gains, vectors, qkv_weight, proj_weight, hidden_weight, hidden_bias, out_weight))) + (bias_table,)

    def forward(field_vals, extra, gains, vecs, qkv_mat, proj_mat, expand_mat, expand_bias, contract_mat, table):

        def pick(layer):
            return (gains[layer], vecs[layer], qkv_mat[layer], proj_mat[layer], expand_mat[layer], expand_bias[layer], contract_mat[layer], table[layer])
        middle = run_layer(field_vals, live_mask, pick(0), False)
        passed = low_back(low(middle)) + extra
        return (run_layer(passed, live_mask, pick(1), True), middle)
    field_vals = images.astype(jnp.float32)
    extra = jnp.zeros_like(field_vals)
    result, pullback, middle = jax.vjp(forward, field_vals, extra, *weights, has_aux=True)
    grads = pullback(out_grad.astype(jnp.float32))
    outputs = jnp.stack([middle, result]).astype(jnp.bfloat16)
    inputs = jnp.stack([grads[0], grads[1]])
    return (outputs, inputs, grads[2], grads[3], grads[4], grads[5], grads[6], grads[7], grads[8], grads[9])
```

```python
import functools
import math

import jax
import jax.numpy as jnp
import numpy as np
from jax import lax
from jax.experimental import pallas as pl
from jax.experimental.pallas import tpu as pltpu
from jax.sharding import PartitionSpec as P

WIN = 7
GRID = 14
SHIFT = 3
TABLE = 169
HEADS = 16
HEAD = 32
D = 512
FF = 2048
TOK = 196
PAD = 208
PAIR = 2
BOTH = PAIR * PAD
WTOK = 64
WINS = 4
ALL = WINS * WTOK
GROUP = 4
GROUPS = HEADS // GROUP
CH = FF // D
BLOCKS = 16
ROWS = D // BLOCKS
QKV_AT, PROJ_AT, HID_AT, OUT_AT, SMALL_AT = 0, 96, 128, 256, 384
PACK_ROWS = 400
GRAD_ROWS = 416
EPS = 1e-05
LOG2E = 1.4426950408889634
SCALE = HEAD**-0.5
LOWEST = -1e30
LIST = 8
VMEM_LIMIT = 60 * 1024 * 1024
SHARDED = ("chip", "core")
SWAP = [(0, 1), (1, 0)]

bf16 = jnp.bfloat16
f32 = jnp.float32


def window_places():
    tables = []
    for shift in (0, SHIFT):
        table = np.full((ALL,), -1, np.int64)
        for window in range(WINS):
            for r in range(WIN):
                for c in range(WIN):
                    row = ((window // 2) * WIN + r + shift) % GRID
                    column = ((window % 2) * WIN + c + shift) % GRID
                    table[window * WTOK + 8 * r + c] = row * GRID + column
        tables.append(table)
    return tables


def permutations():
    mats = []
    for table in window_places():
        mat = np.zeros((ALL, PAD), np.float32)
        for at, token in enumerate(table):
            if token >= 0:
                mat[at, token] = 1.0
        mats.append(mat)
    return mats


def pair_offsets():
    place = np.arange(WTOK)
    r, c = place // 8, place % 8
    real = (r < WIN) & (c < WIN)
    offset = (r[None, :] - r[:, None] + WIN - 1) * (2 * WIN - 1) + c[None, :] - c[:, None] + WIN - 1
    return np.where(real[None, :] & real[:, None], offset, -1)


def region_masks():
    line = np.arange(GRID)
    band = (line >= GRID - WIN).astype(int) + (line >= GRID - SHIFT).astype(int)
    out = np.zeros((WINS, WTOK, WTOK), np.float32)
    for window in range(WINS):
        ids = np.full((WTOK,), -1)
        for r in range(WIN):
            for c in range(WIN):
                ids[8 * r + c] = (
                    3 * band[(window // 2) * WIN + r] + band[(window % 2) * WIN + c]
                )
        out[window] = np.where(ids[:, None] != ids[None, :], -100.0, 0.0)
    return out


def bias_arrays(table, masked):
    offsets = pair_offsets()
    pick = jnp.asarray(offsets.reshape(-1, 1), jnp.int32) == jnp.arange(TABLE, dtype=jnp.int32)[None, :]
    flat = jnp.dot(pick.astype(f32), table, precision=lax.Precision.HIGHEST)
    bias = flat.reshape(WTOK, WTOK, GROUPS, GROUP).transpose(2, 0, 3, 1)
    if masked:
        bias = bias[None] + jnp.asarray(region_masks())[:, None, :, None, :]
    else:
        bias = bias[None]
    place = np.arange(WTOK)
    real_key = (place // 8 < WIN) & (place % 8 < WIN)
    bias = jnp.where(jnp.asarray(real_key)[None, None, :, None, None], bias * LOG2E, LOWEST)
    return bias.reshape(bias.shape[0], GROUPS, WTOK, GROUP * WTOK)


def dot(a, b):
    return jnp.dot(a, b, preferred_element_type=f32)


def dot_nt(a, b):
    return lax.dot_general(a, b, (((1,), (1,)), ((), ())), preferred_element_type=f32)


def dot_tn(a, b):
    return lax.dot_general(a, b, (((0,), (0,)), ((), ())), preferred_element_type=f32)


def block(w_ref, at):
    return w_ref[:, pl.ds(at, ROWS), :].reshape(D, D)


def out_block(w_ref, k):
    return w_ref[pl.ds(k * (BLOCKS // CH), BLOCKS // CH), OUT_AT:SMALL_AT, :].reshape(D, D)


def normalize(values):
    center = values - jnp.mean(values, axis=-1, keepdims=True)
    inverse = lax.rsqrt(jnp.mean(center * center, axis=-1, keepdims=True) + EPS)
    return center * inverse, inverse


def norm_backward(grad_hat, hat, inverse):
    mean = jnp.mean(grad_hat, axis=-1, keepdims=True)
    along = jnp.mean(grad_hat * hat, axis=-1, keepdims=True)
    return inverse * (grad_hat - mean - hat * along)


ERF_T = 0.3275911
ERF_C = (0.254829592, -0.284496736, 1.421413741, -1.453152027, 1.061405429)


def gelu_and_slope(u):
    u = u.astype(bf16)
    size = jnp.abs(u)
    t = pltpu.reciprocal(size * bf16(ERF_T * 0.5**0.5) + bf16(1.0), approx=True)
    bell = jnp.exp2(u * u * bf16(-0.5 * LOG2E))
    tail = bf16(0.5 * ERF_C[4])
    for c in ERF_C[3::-1]:
        tail = tail * t + bf16(0.5 * c)
    tail = tail * t * bell
    phi = jnp.where(u >= bf16(0.0), bf16(1.0) - tail, tail)
    return jnp.maximum(u, bf16(0.0)) - size * tail, phi + u * bell * bf16((0.5 / math.pi) ** 0.5)


def head_masks():
    lane_head = lax.broadcasted_iota(jnp.int32, (WTOK, GROUP * HEAD), 1) // HEAD
    return [(lane_head == h).astype(f32).astype(bf16) for h in range(GROUP)]


def spread_heads(tile, masks):
    return jnp.concatenate([tile * mask for mask in masks], axis=0)


def put_diagonal(out_ref, image, group, pair, even, odd):
    for h in range(GROUP):
        rows, lanes = slice(h * HEAD, (h + 1) * HEAD), slice(h * WTOK, (h + 1) * WTOK)
        both = jnp.concatenate([even[rows, lanes], odd[rows, lanes]], axis=1)
        at = group * GROUP * HEAD + h * HEAD
        out_ref[image, at : at + HEAD, pair * 128 : (pair + 1) * 128] = both.astype(bf16)


def tiles_of(pair, group):
    lanes = slice(group * GROUP * HEAD, (group + 1) * GROUP * HEAD)
    for image in range(PAIR):
        for window in (2 * pair, 2 * pair + 1):
            at = image * ALL + window * WTOK
            yield image, window, slice(at, at + WTOK), lanes


def attention_forward(q_ref, k_ref, v_ref, p_ref, ot_ref, bias_ref):
    masks = head_masks()
    bias_windows = bias_ref.shape[0]
    for pair in range(WINS // 2):
        for group in range(GROUPS):
            tiles = list(tiles_of(pair, group))
            scores = [
                dot_nt(k_ref[rows, lanes], spread_heads(q_ref[rows, lanes], masks)) * (SCALE * LOG2E)
                + bias_ref[window if bias_windows > 1 else 0, group]
                for _, window, rows, lanes in tiles
            ]
            tops = [jnp.max(tile, axis=0, keepdims=True) for tile in scores]
            powers = [jnp.exp2(tile - top) for tile, top in zip(scores, tops)]
            totals = [1.0 / jnp.sum(tile, axis=0, keepdims=True) for tile in powers]
            probs = [(tile * total).astype(bf16) for tile, total in zip(powers, totals)]
            for (image, window, _, _), tile in zip(tiles, probs):
                p_ref[image, window, group] = tile
            products = [
                dot_tn(v_ref[rows, lanes], tile) for (_, _, rows, lanes), tile in zip(tiles, probs)
            ]
            for image in range(PAIR):
                put_diagonal(ot_ref, image, group, pair, *products[2 * image : 2 * image + 2])


def attention_backward(q_ref, k_ref, v_ref, p_ref, do_ref, dqt_ref, dk_ref, dv_ref, score_ref):
    masks = head_masks()
    for pair in range(WINS // 2):
        for group in range(GROUPS):
            tiles = list(tiles_of(pair, group))
            spreads = [spread_heads(do_ref[rows, lanes], masks) for _, _, rows, lanes in tiles]
            probs = [p_ref[image, window, group] for image, window, _, _ in tiles]
            grad_probs = [
                dot_nt(v_ref[rows, lanes], spread) for (_, _, rows, lanes), spread in zip(tiles, spreads)
            ]
            for (_, _, rows, lanes), tile, spread in zip(tiles, probs, spreads):
                dv_ref[rows, lanes] = dot(tile, spread).astype(bf16)
            weighted = [tile * prob.astype(f32) for tile, prob in zip(grad_probs, probs)]
            sums = [jnp.sum(tile, axis=0, keepdims=True) for tile in weighted]
            grads = [
                tile - prob.astype(f32) * total for tile, prob, total in zip(weighted, probs, sums)
            ]
            score_ref[group] += (grads[0] + grads[1]) + (grads[2] + grads[3])
            lows = [tile.astype(bf16) for tile in grads]
            for (_, _, rows, lanes), low in zip(tiles, lows):
                queries = spread_heads(q_ref[rows, lanes], masks)
                dk_ref[rows, lanes] = (dot(low, queries) * SCALE).astype(bf16)
            products = [
                dot_tn(k_ref[rows, lanes], low) * SCALE for (_, _, rows, lanes), low in zip(tiles, lows)
            ]
            for image in range(PAIR):
                put_diagonal(dqt_ref, image, group, pair, *products[2 * image : 2 * image + 2])


def to_windows(perm_ref, rows):
    return jnp.concatenate(
        [dot(perm_ref[...], rows[i * PAD : (i + 1) * PAD]).astype(bf16) for i in range(PAIR)], axis=0
    )


def from_windows(perm_t_ref, ref):
    return jnp.concatenate(
        [dot(perm_t_ref[...], ref[i * ALL : (i + 1) * ALL, :]) for i in range(PAIR)], axis=0
    )


def from_windows_turned(perm_t_ref, ref):
    return jnp.concatenate([dot_nt(perm_t_ref[...], ref[i]) for i in range(PAIR)], axis=0)


def forward_part(x_ref, w_ref, small_ref, perm_ref, perm_t_ref, bias_ref, a):
    hat1, inv1 = normalize(x_ref[...])
    norm1 = (hat1 * small_ref[0:1, :] + small_ref[2:3, :]).astype(bf16)
    blocks = to_windows(perm_ref, norm1)
    a["q"][...] = (dot(blocks, block(w_ref, QKV_AT)) + small_ref[3:4, :]).astype(bf16)
    a["k"][...] = dot(blocks, block(w_ref, QKV_AT + ROWS)).astype(bf16)
    a["v"][...] = (dot(blocks, block(w_ref, QKV_AT + 2 * ROWS)) + small_ref[4:5, :]).astype(bf16)
    attention_forward(a["q"], a["k"], a["v"], a["p"], a["ot"], bias_ref)
    mixed = from_windows_turned(perm_t_ref, a["ot"]).astype(bf16)
    resid = x_ref[...] + dot(mixed, block(w_ref, PROJ_AT)) + small_ref[5:6, :]
    a["resid"][...] = resid
    hat2, inv2 = normalize(resid)
    norm2 = (hat2 * small_ref[1:2, :] + small_ref[6:7, :]).astype(bf16)
    a["n2"][...] = norm2
    a["h"][...] = resid + small_ref[7:8, :]

    def chunk(k):
        hidden = dot(a["n2"][...], block(w_ref, HID_AT + k * ROWS)) + small_ref[pl.ds(8 + k, 1), :]
        active, slope = gelu_and_slope(hidden)
        a["g"][k] = active
        a["slope"][k] = slope
        a["h"][...] += dot(active, out_block(w_ref, k))

    for k in range(CH):
        chunk(k)
    return hat1, inv1, norm1, hat2, inv2


def add_rows(ref, at, values):
    ref[at] += jnp.sum(values.reshape(BOTH // 8, 8, D), axis=0)


def backward_part(e_ref, hats, w_ref, small_ref, perm_ref, perm_t_ref, a, b):
    hat1, inv1, norm1, hat2, inv2 = hats

    def back(rows, at):
        if at < 4 + CH:
            return dot_nt(rows, block(w_ref, at * ROWS))
        return dot_nt(rows, out_block(w_ref, at - 4 - CH))

    out_grad = e_ref[...].astype(bf16)
    add_rows(b["rows"], 7, out_grad.astype(f32))
    b["dz"][...] = out_grad
    b["dzt"][...] = out_grad.T
    b["n2t"][...] = a["n2"][...].T
    b["dn2"][...] = jnp.zeros((BOTH, D), f32)

    def chunk(k):
        grad_hidden = back(b["dz"][...], 4 + CH + k) * a["slope"][k].astype(f32)
        b["rows"][8 + k] += jnp.sum(grad_hidden.reshape(BOTH // 8, 8, D), axis=0)
        low = grad_hidden.astype(bf16)
        b["dn2"][...] += back(low, 4 + k)
        at = pl.ds(HID_AT + k * ROWS, ROWS)
        b["acc"][:, at, :] += dot(b["n2t"][...], low).reshape(BLOCKS, ROWS, D)
        b["acc_out"][k] += dot(b["dzt"][...], a["g"][k])

    for k in range(CH):
        chunk(k)
    dn2 = b["dn2"][...]
    add_rows(b["rows"], 1, dn2 * hat2)
    add_rows(b["rows"], 6, dn2)
    dr = e_ref[...] + norm_backward(dn2 * small_ref[1:2, :], hat2, inv2)
    low = dr.astype(bf16)
    add_rows(b["rows"], 5, low.astype(f32))
    attn = to_windows(perm_ref, low)
    b["do"][...] = back(attn, 3).astype(bf16)
    proj = dot(a["ot"][0], attn[:ALL]) + dot(a["ot"][1], attn[ALL:])
    b["acc"][:, PROJ_AT : PROJ_AT + ROWS, :] += proj.reshape(BLOCKS, ROWS, D)
    attention_backward(
        a["q"], a["k"], a["v"], a["p"], b["do"], b["dqt"], b["dk"], b["dv"], b["scores"]
    )
    norm1_t = norm1.T
    dn1 = jnp.zeros((BOTH, D), f32)
    for at in range(3):
        if at == 0:
            rows = from_windows_turned(perm_t_ref, b["dqt"])
        else:
            rows = from_windows(perm_t_ref, b["dk" if at == 1 else "dv"])
        if at != 1:
            add_rows(b["rows"], 3 + at // 2, rows)
        rows = rows.astype(bf16)
        dn1 = dn1 + back(rows, at)
        take = slice(QKV_AT + at * ROWS, QKV_AT + (at + 1) * ROWS)
        b["acc"][:, take, :] += dot(norm1_t, rows).reshape(BLOCKS, ROWS, D)
    add_rows(b["rows"], 0, dn1 * hat1)
    add_rows(b["rows"], 2, dn1)
    return dr + norm_backward(dn1 * small_ref[0:1, :], hat1, inv1)


def clear_sums(b):
    for name in ("acc", "acc_out", "rows", "scores"):
        b[name][...] = jnp.zeros(b[name].shape, f32)


def table_rows(score_ref, fold_ref):
    lane = lax.broadcasted_iota(jnp.int32, (WTOK, 128), 1)
    for head in range(HEADS):
        group, h = head // GROUP, head % GROUP
        tile = score_ref[group, :, 128 * (h // 2) : 128 * (h // 2) + 128]
        if h % 2:
            tile = pltpu.roll(tile, WTOK, 1)
        tile = jnp.where(lane < WTOK, tile, 0.0)
        total = jnp.zeros((8, 128), f32)
        for r in range(WIN):
            turned = tile[8 * r : 8 * r + 8]
            if r < WIN - 1:
                turned = pltpu.roll(turned, 8 * (WIN - 1 - r), 1)
            total = total + turned
        fold_ref[8 * head : 8 * head + 8, :] = total
    lane = lax.broadcasted_iota(jnp.int32, (128, 256), 0)
    goal = lax.broadcasted_iota(jnp.int32, (128, 256), 1)
    out = jnp.zeros((HEADS, 256), f32)
    for c in range(WIN):
        pick = (goal == 16 * (lane // 8) + lane % 8 - c + WIN - 1) & (lane % 8 < WIN)
        out = out + jnp.dot(
            fold_ref[pl.ds(c, HEADS, stride=8), :],
            pick.astype(f32),
            precision=lax.Precision.HIGHEST,
            preferred_element_type=f32,
        )
    return out


def write_sums(b, fold_ref, put):
    everything = slice(0, D)
    width = FF // BLOCKS
    for owner in range(BLOCKS):
        k, lane = owner // (BLOCKS // CH), width * (owner % (BLOCKS // CH))
        put(owner, slice(0, OUT_AT), everything, lambda: b["acc"][owner].astype(bf16))
        for at in range(D // width):
            lanes = slice(at * width, (at + 1) * width)
            put(
                owner,
                slice(OUT_AT, SMALL_AT),
                lanes,
                lambda: b["acc_out"][k, lanes, lane : lane + width].astype(bf16),
            )
    rows = jnp.sum(b["rows"][...], axis=1)
    rows = jnp.concatenate([rows, jnp.zeros((4, D), f32)], axis=0).astype(bf16)
    table = table_rows(b["scores"], fold_ref)
    table = jnp.concatenate([table, jnp.zeros((HEADS, D - 256), f32)], axis=1).astype(bf16)
    for owner in range(BLOCKS):
        put(owner, slice(SMALL_AT, PACK_ROWS), everything, lambda: rows)
        put(owner, slice(PACK_ROWS, GRAD_ROWS), everything, lambda: table)


def sum_small(w_ref, small_ref):
    small_ref[...] = jnp.sum(w_ref[:, SMALL_AT:PACK_ROWS, :].astype(f32), axis=0)


KEPT = {
    "q": ((PAIR * ALL, D), bf16),
    "k": ((PAIR * ALL, D), bf16),
    "v": ((PAIR * ALL, D), bf16),
    "p": ((PAIR, WINS, GROUPS, WTOK, GROUP * WTOK), bf16),
    "ot": ((PAIR, D, ALL), bf16),
    "resid": ((BOTH, D), f32),
    "g": ((CH, BOTH, D), bf16),
    "slope": ((CH, BOTH, D), bf16),
}
LOCAL_F = {"n2": ((BOTH, D), bf16), "h": ((BOTH, D), f32)}
LOCAL_B = {
    "acc": ((BLOCKS, OUT_AT, D), f32),
    "acc_out": ((CH, D, D), f32),
    "rows": ((12, 8, D), f32),
    "scores": ((GROUPS, WTOK, GROUP * WTOK), f32),
    "dz": ((BOTH, D), bf16),
    "dzt": ((D, BOTH), bf16),
    "n2t": ((D, BOTH), bf16),
    "dn2": ((BOTH, D), f32),
    "do": ((PAIR * ALL, D), bf16),
    "dqt": ((PAIR, D, ALL), bf16),
    "dk": ((PAIR * ALL, D), bf16),
    "dv": ((PAIR * ALL, D), bf16),
}


def scratch(shapes):
    return [pltpu.VMEM(shape, dtype) for shape, dtype in shapes.values()]


def load_images(goal_ref, where_ref, step, refs):
    for image in range(PAIR):
        at = PAIR * step + image
        rows = slice(image * PAD, image * PAD + TOK)
        for core in range(2):

            @pl.when((at < where_ref[0]) & (where_ref[1 + at] // where_ref[1 + LIST] == core))
            def _():
                goal_ref[rows, :] = refs[2 * image + core][0, 0].astype(f32)

        @pl.when(at >= where_ref[0])
        def _():
            goal_ref[rows, :] = jnp.zeros((TOK, D), f32)


def load_rows(goal_ref, ref):
    for image in range(PAIR):
        goal_ref[image * PAD : image * PAD + TOK, :] = ref[image, 0:TOK, :].astype(f32)


def store_sides(own_ref, send_ref, where_ref, first, second):
    for section in range(2):

        @pl.when(where_ref[4 + LIST] == section)
        def _():
            own_ref[...] = second if section else first
            send_ref[...] = first if section else second


def store_rows(ref, values):
    for image in range(PAIR):
        ref[image] = values[image * PAD : (image + 1) * PAD].astype(bf16)


def first_kernel(where_ref, x0, x1, x2, x3, w_ref, perm_ref, perm_t_ref, bias_ref, h_ref, *refs):
    kept = dict(zip(KEPT, refs))
    refs = refs[len(KEPT) :]
    kept.update(zip(LOCAL_F, refs))
    xs_ref, small_ref = refs[len(LOCAL_F) :]
    kept = {name: (ref.at[0] if name in KEPT else ref) for name, ref in kept.items()}
    step = pl.program_id(0)

    @pl.when(step == 0)
    def _():
        xs_ref[...] = jnp.zeros(xs_ref.shape, f32)
        sum_small(w_ref, small_ref)

    @pl.when(PAIR * step < where_ref[0])
    def _():
        load_images(xs_ref, where_ref, step, (x0, x1, x2, x3))
        forward_part(xs_ref, w_ref, small_ref, perm_ref, perm_t_ref, bias_ref, kept)
        store_rows(h_ref, kept["h"][...])


def second_kernel(
    where_ref,
    x_ref,
    e0,
    e1,
    e2,
    e3,
    w_ref,
    perm_ref,
    perm_t_ref,
    bias_ref,
    own_ref,
    send_ref,
    ig_ref,
    gp_ref,
    *refs,
):
    names = {**KEPT, **LOCAL_F}
    kept = dict(zip(names, refs))
    refs = refs[len(names) :]
    sums = dict(zip(LOCAL_B, refs))
    xs_ref, es_ref, small_ref, fold_ref = refs[len(LOCAL_B) :]
    step = pl.program_id(0)

    @pl.when(step == 0)
    def _():
        xs_ref[...] = jnp.zeros(xs_ref.shape, f32)
        es_ref[...] = jnp.zeros(es_ref.shape, f32)
        sum_small(w_ref, small_ref)
        clear_sums(sums)

    @pl.when(PAIR * step < where_ref[0])
    def _():
        load_rows(xs_ref, x_ref)
        load_images(es_ref, where_ref, step, (e0, e1, e2, e3))
        hats = forward_part(xs_ref, w_ref, small_ref, perm_ref, perm_t_ref, bias_ref, kept)
        out = kept["h"][...].reshape(PAIR, PAD, D).astype(bf16)
        store_sides(own_ref, send_ref, where_ref, x_ref[...], out)
        grad = backward_part(es_ref, hats, w_ref, small_ref, perm_ref, perm_t_ref, kept, sums)
        store_rows(ig_ref, grad)

    @pl.when(step == pl.num_programs(0) - 1)
    def _():
        def put(owner, rows, lanes, values):
            gp_ref[owner, rows, lanes] = values()

        write_sums(sums, fold_ref, put)


def third_kernel(where_ref, x0, x1, x2, x3, e_ref, w_ref, perm_ref, perm_t_ref, *refs):
    kept = {name: ref.at[0] for name, ref in zip(KEPT, refs)}
    own_ref, other_ref, keep_ref, send_ref = refs[len(KEPT) : len(KEPT) + 4]
    refs = refs[len(KEPT) + 4 :]
    sums = dict(zip(LOCAL_B, refs))
    n2_ref, xs_ref, es_ref, small_ref, fold_ref = refs[len(LOCAL_B) :]
    kept["n2"] = n2_ref
    step = pl.program_id(0)

    @pl.when(step == 0)
    def _():
        xs_ref[...] = jnp.zeros(xs_ref.shape, f32)
        es_ref[...] = jnp.zeros(es_ref.shape, f32)
        sum_small(w_ref, small_ref)
        clear_sums(sums)

    @pl.when(PAIR * step < where_ref[0])
    def _():
        load_images(xs_ref, where_ref, step, (x0, x1, x2, x3))
        load_rows(es_ref, e_ref)
        hat1, inv1 = normalize(xs_ref[...])
        norm1 = (hat1 * small_ref[0:1, :] + small_ref[2:3, :]).astype(bf16)
        hat2, inv2 = normalize(kept["resid"][...])
        n2_ref[...] = (hat2 * small_ref[1:2, :] + small_ref[6:7, :]).astype(bf16)
        hats = (hat1, inv1, norm1, hat2, inv2)
        grad = backward_part(es_ref, hats, w_ref, small_ref, perm_ref, perm_t_ref, kept, sums)
        out = grad.reshape(PAIR, PAD, D).astype(bf16)
        store_sides(own_ref, other_ref, where_ref, out, e_ref[...])

    @pl.when(step == pl.num_programs(0) - 1)
    def _():
        for core in range(2):

            @pl.when(where_ref[2 + LIST] == core)
            def _():
                def put(owner, rows, lanes, values):
                    goal_ref = keep_ref if owner % 2 == core else send_ref
                    goal_ref[owner // 2, rows, lanes] = values()

                write_sums(sums, fold_ref, put)


def spread_kernel(flags_ref, *refs):
    out_ref, held_ref = refs[-2:]
    slots = out_ref.shape[2]
    for slot in range(slots):
        kind = flags_ref[pl.program_id(0) * slots + slot]
        for at in range(4):

            @pl.when(kind == at)
            def _():
                held_ref[slot] = refs[4 * slot + at][0]

        @pl.when(kind == 4)
        def _():
            held_ref[slot] = jnp.zeros(held_ref.shape[1:], held_ref.dtype)

    values = [held_ref[slot, 0:TOK, :].astype(out_ref.dtype) for slot in range(slots)]
    if out_ref.dtype == f32:
        for slot in range(slots):
            out_ref[0, :, slot, :] = values[slot]
    else:
        out_ref[0] = jnp.stack(values, axis=1)


def whole(array):
    zeros = (0,) * array.ndim
    return pl.BlockSpec(array.shape, lambda *_: zeros, pipeline_mode=pl.Buffered(1))


def of_layer(weights, layer):
    return pl.BlockSpec(
        (None, *weights.shape[1:]), lambda *_: (layer, 0, 0, 0), pipeline_mode=pl.Buffered(1)
    )


def params():
    return pltpu.CompilerParams(vmem_limit_bytes=VMEM_LIMIT, dimension_semantics=("arbitrary",))


def cost(images, layers):
    return pl.CostEstimate(
        flops=int(images * layers * 1.6e9), bytes_accessed=int(images * 4e6), transcendentals=int(images * 1e6)
    )


def live_step(k, where):
    return jnp.minimum(k, (where[0] - 1) // PAIR)


def by_step(shape):
    zeros = (0,) * len(shape)
    return pl.BlockSpec((1, *shape), lambda k, where: (live_step(k, where), *zeros))


def by_pair():
    return pl.BlockSpec((PAIR, PAD, D), lambda k, where: (live_step(k, where), 0, 0))


def by_image(micro, slots):
    def spec(image, core):
        def at(k, where):
            found = jnp.int32(0)
            for earlier in range(LIST // PAIR):
                entry = where[1 + PAIR * earlier + image]
                use = (earlier <= k) & (entry // (micro * slots) == core)
                found = jnp.where(use, entry % (micro * slots), found)
            return (found // slots, found % slots, 0, 0)

        return pl.BlockSpec((1, 1, TOK, D), at)

    return [spec(image, core) for image in range(PAIR) for core in range(2)]


def run_first(where, images, others, weights, perm, perm_t, bias):
    steps = LIST // PAIR
    outs = list(KEPT.values())
    return pl.pallas_call(
        first_kernel,
        grid_spec=pltpu.PrefetchScalarGridSpec(
            num_scalar_prefetch=1,
            grid=(steps,),
            in_specs=by_image(*images.shape[:2])
            + [of_layer(weights, 0)]
            + [whole(array) for array in (perm, perm_t, bias)],
            out_specs=[by_pair()] + [by_step(shape) for shape, _ in outs],
            scratch_shapes=scratch(LOCAL_F) + [pltpu.VMEM((BOTH, D), f32), pltpu.VMEM((16, D), f32)],
        ),
        out_shape=[IMAGES]
        + [jax.ShapeDtypeStruct((steps, *shape), dtype) for shape, dtype in outs],
        compiler_params=params(),
        cost_estimate=cost(LIST, 1),
        name="layer0_forward",
    )(where, images, others, images, others, weights, perm, perm_t, bias)


IMAGES = jax.ShapeDtypeStruct((LIST, PAD, D), bf16)
GRADS = jax.ShapeDtypeStruct((BLOCKS, GRAD_ROWS, D), bf16)
HALF = jax.ShapeDtypeStruct((BLOCKS // 2, GRAD_ROWS, D), bf16)


def run_second(where, rows, out_grad, others, weights, perm, perm_t, bias):
    return pl.pallas_call(
        second_kernel,
        grid_spec=pltpu.PrefetchScalarGridSpec(
            num_scalar_prefetch=1,
            grid=(LIST // PAIR,),
            in_specs=[by_pair()]
            + by_image(*out_grad.shape[:2])
            + [of_layer(weights, 1)]
            + [whole(array) for array in (perm, perm_t, bias)],
            out_specs=[by_pair(), by_pair(), by_pair(), whole(GRADS)],
            scratch_shapes=scratch({**KEPT, **LOCAL_F})
            + scratch(LOCAL_B)
            + [
                pltpu.VMEM((BOTH, D), f32),
                pltpu.VMEM((BOTH, D), f32),
                pltpu.VMEM((16, D), f32),
                pltpu.VMEM((128, 128), f32),
            ],
        ),
        out_shape=[IMAGES, IMAGES, IMAGES, GRADS],
        compiler_params=params(),
        cost_estimate=cost(LIST, 3),
        name="layer1_both",
    )(where, rows, out_grad, others, out_grad, others, weights, perm, perm_t, bias)


def run_third(where, images, others, grads, weights, perm, perm_t, kept):
    return pl.pallas_call(
        third_kernel,
        grid_spec=pltpu.PrefetchScalarGridSpec(
            num_scalar_prefetch=1,
            grid=(LIST // PAIR,),
            in_specs=by_image(*images.shape[:2])
            + [by_pair(), of_layer(weights, 0), whole(perm), whole(perm_t)]
            + [by_step(shape) for shape, _ in KEPT.values()],
            out_specs=[by_pair(), by_pair(), whole(HALF), whole(HALF)],
            scratch_shapes=scratch(LOCAL_B)
            + [
                pltpu.VMEM((BOTH, D), bf16),
                pltpu.VMEM((BOTH, D), f32),
                pltpu.VMEM((BOTH, D), f32),
                pltpu.VMEM((16, D), f32),
                pltpu.VMEM((128, 128), f32),
            ],
        ),
        out_shape=[IMAGES, IMAGES, HALF, HALF],
        compiler_params=params(),
        cost_estimate=cost(LIST, 2),
        name="layer0_backward",
    )(where, images, others, images, others, grads, weights, perm, perm_t, *kept)


def run_spread(flags, lists, micro, slots, dtype):
    def spec(slot, kind):
        def at(m, flags):
            i = m * slots + slot
            return (jnp.where(flags[i] == kind, flags[micro * slots + i], 0), 0, 0)

        return pl.BlockSpec((1, PAD, D), at)

    return pl.pallas_call(
        spread_kernel,
        grid_spec=pltpu.PrefetchScalarGridSpec(
            num_scalar_prefetch=1,
            grid=(micro,),
            in_specs=[spec(slot, kind) for slot in range(slots) for kind in range(4)],
            out_specs=pl.BlockSpec((1, TOK, slots, D), lambda m, flags: (m, 0, 0, 0)),
            scratch_shapes=[pltpu.VMEM((slots, PAD, D), bf16)],
        ),
        out_shape=jax.ShapeDtypeStruct((micro, TOK, slots, D), dtype),
        compiler_params=params(),
        name="spread_images",
    )(flags, *(list(lists) * slots))


def add_kernel(chip_ref, keep_ref, got_ref, *out_refs):
    chips = len(out_refs)
    for d, out_ref in enumerate(out_refs):
        at = lax.rem(chip_ref[0] + d, chips)
        out_ref[...] = (keep_ref[at].astype(f32) + got_ref[at].astype(f32)).astype(bf16)


def run_add(chip, keep, got):
    chips = keep.shape[0]
    one = jax.ShapeDtypeStruct((GRAD_ROWS, D), bf16)
    in_vmem = pl.BlockSpec(memory_space=pltpu.VMEM)
    return pl.pallas_call(
        add_kernel,
        grid_spec=pltpu.PrefetchScalarGridSpec(
            num_scalar_prefetch=1,
            grid=(),
            in_specs=[in_vmem] * 2,
            out_specs=[in_vmem] * chips,
        ),
        out_shape=[one] * chips,
        compiler_params=pltpu.CompilerParams(vmem_limit_bytes=VMEM_LIMIT),
        name="add_cores",
    )(chip.reshape(1).astype(jnp.int32), keep, got)


def parts_kernel(section_ref, first_ref, *refs):
    own_ref, send_ref = refs[-2:]
    total = refs[0][...].astype(f32)
    for ref in refs[1:-2]:
        total = total + ref[...].astype(f32)
    total = total.astype(bf16)
    for section in range(2):

        @pl.when(section_ref[0] == section)
        def _():
            own_ref[...] = first_ref[...] if section else total
            send_ref[...] = total if section else first_ref[...]


def run_parts(section, sums1, parts):
    one = jax.ShapeDtypeStruct(sums1.shape, bf16)
    spec = pl.BlockSpec((sums1.shape[0] // 2, D), lambda i, section: (i, 0))
    return pl.pallas_call(
        parts_kernel,
        grid_spec=pltpu.PrefetchScalarGridSpec(
            num_scalar_prefetch=1,
            grid=(2,),
            in_specs=[spec] * (1 + len(parts)),
            out_specs=[spec] * 2,
        ),
        out_shape=[one] * 2,
        compiler_params=params(),
        name="add_chips",
    )(section.reshape(1).astype(jnp.int32), sums1, *parts)


def final_kernel(place_ref, *refs):
    own_ref, got_ref, *out_refs, total_ref = refs
    gains_ref, vectors_ref, qkv_ref, proj_ref, hidden_ref, bias_ref, out_ref, table_ref = out_refs
    total_ref[...] = own_ref[...].astype(f32) + got_ref[...].astype(f32)
    index = place_ref[0]
    rows, width = qkv_ref.shape[0], out_ref.shape[0]
    for at in range(3):
        qkv_ref[:, at * D : (at + 1) * D] = total_ref[at * rows : (at + 1) * rows, :]
    proj_ref[...] = total_ref[3 * rows : 4 * rows, :]
    for at in range(CH):
        hidden_ref[:, at * D : (at + 1) * D] = total_ref[(4 + at) * rows : (5 + at) * rows, :]
    if width == FF // BLOCKS:
        for at in range(D // width):
            lanes = slice(at * width, (at + 1) * width)
            out_ref[:, lanes] = total_ref[8 * rows : 8 * rows + width, lanes].T
    else:
        out_ref[...] = total_ref[8 * rows : 8 * rows + width, :]
    small = total_ref[8 * rows + width : 8 * rows + width + 16, :]
    own = pltpu.roll(small, D - index * rows, 1)
    gains_ref[...] = own[0:2, :rows]
    for at in range(6):
        vectors_ref[at] = own[2 + at : 3 + at, :rows]
    row = lax.broadcasted_iota(jnp.int32, (16, D), 0)
    mine = jnp.where(row == 8 + index * width // D, small, 0.0)
    mine = jnp.sum(mine, axis=0, keepdims=True)
    mine = pltpu.roll(jnp.broadcast_to(mine, (8, D)), D - lax.rem(index * width, D), 1)
    bias_ref[...] = mine[0:1, :width]
    side = 2 * WIN - 1
    goal = lax.broadcasted_iota(jnp.int32, (TABLE, 256), 0)
    lane = lax.broadcasted_iota(jnp.int32, (TABLE, 256), 1)
    pick = (lane == 16 * (goal // side) + lax.rem(goal, side)).astype(f32)
    table = total_ref[8 * rows + width + 16 : 8 * rows + width + 32, 0:256]
    table_ref[...] = lax.dot_general(
        table,
        pick,
        (((1,), (1,)), ((), ())),
        precision=lax.Precision.HIGHEST,
        preferred_element_type=f32,
    )


def run_final(index, own, got, shards):
    rows, width = D // shards, FF // shards
    shapes = [
        (2, rows), (6, 1, rows), (rows, 3 * D), (rows, D), (rows, FF), (1, width), (width, D), (HEADS, TABLE)
    ]
    outs = pl.pallas_call(
        final_kernel,
        grid_spec=pltpu.PrefetchScalarGridSpec(
            num_scalar_prefetch=1,
            grid=(),
            in_specs=[pl.BlockSpec(memory_space=pltpu.VMEM)] * 2,
            out_specs=[pl.BlockSpec(memory_space=pltpu.VMEM)] * 8,
            scratch_shapes=[pltpu.VMEM(own.shape, f32)],
        ),
        out_shape=[jax.ShapeDtypeStruct(shape, f32) for shape in shapes],
        name="final_sums",
    )(index.reshape(1).astype(jnp.int32), own, got)
    outs = list(outs)
    outs[1] = outs[1].reshape(6, rows)
    outs[5] = outs[5].reshape(width)
    outs[7] = outs[7].T
    return outs


def pack_kernel(qkv_ref, proj_ref, hidden_ref, out_ref, small_ref, packed_ref):
    rows = qkv_ref.shape[0]
    for at in range(3):
        packed_ref[at * rows : (at + 1) * rows, :] = qkv_ref[:, at * D : (at + 1) * D]
    packed_ref[3 * rows : 4 * rows, :] = proj_ref[...]
    for at in range(CH):
        packed_ref[(4 + at) * rows : (5 + at) * rows, :] = hidden_ref[:, at * D : (at + 1) * D]
    width = out_ref.shape[0]
    packed_ref[8 * rows : 8 * rows + width, :] = out_ref[...]
    packed_ref[8 * rows + width : 8 * rows + width + 16, :] = small_ref[...]


def pack_weights(norm_gains, vectors, qkv, proj, hidden, hidden_bias, out, index, shards):
    small = jnp.concatenate([norm_gains[0], vectors[0]], axis=0)
    mine = jnp.arange(shards)[None, :, None] == index
    small = jnp.where(mine, small[:, None, :], jnp.zeros((), bf16)).reshape(8, D)
    bias = jnp.where(mine[0], hidden_bias, jnp.zeros((), bf16)).reshape(CH, D)
    small = jnp.concatenate([small, bias, jnp.zeros((4, D), bf16)], axis=0)
    rows = 8 * qkv.shape[1] + out.shape[1] + 16
    return pl.pallas_call(
        pack_kernel, out_shape=jax.ShapeDtypeStruct((rows, D), bf16), name="pack_weights"
    )(qkv[0], proj[0], hidden[0], out[0], small)


def regroup(array, rows_from, rows_to, goal):
    pieces, at = [], 0
    for rows, new_rows in zip(rows_from, rows_to):
        pieces.append(array[:, at : at + rows].reshape(goal, new_rows, D))
        at += rows
    return pieces


def merge_shards(gathered, shards):
    rows = D // shards
    parts = [rows] * 8 + [FF // shards]
    goals = [ROWS] * 8 + [FF // BLOCKS]
    pieces = regroup(gathered[:, : sum(parts)], parts, goals, BLOCKS)
    small = jnp.sum(gathered[:, sum(parts) :].astype(f32), axis=0).astype(bf16)
    small = jnp.where(jnp.arange(BLOCKS)[:, None, None] == 0, small[None], jnp.zeros((), bf16))
    return jnp.concatenate(pieces + [small], axis=1)


def shift(array, by):
    chips = lax.axis_size("chip")
    return lax.ppermute(array, "chip", [(i, (i + by) % chips) for i in range(chips)])


def split_shards(packed, shards):
    if shards == BLOCKS:
        return packed
    rows, width = D // shards, FF // BLOCKS
    parts = [ROWS] * 8 + [width]
    goals = [rows] * 8 + [FF // shards]
    turned = packed[:, OUT_AT:SMALL_AT].reshape(BLOCKS, width, D // width, width)
    turned = turned.transpose(0, 3, 2, 1).reshape(BLOCKS, width, D)
    blocks = jnp.concatenate([packed[:, :OUT_AT], turned], axis=1)
    pieces = regroup(blocks, parts, goals, shards)
    small = jnp.broadcast_to(packed[:1, SMALL_AT:], (shards, GRAD_ROWS - SMALL_AT, D))
    return jnp.concatenate(pieces + [small], axis=1)


def on_device(
    images,
    live_counts,
    norm_gains,
    vectors,
    qkv_weight,
    proj_weight,
    hidden_weight,
    hidden_bias,
    out_weight,
    bias_table,
    out_grad,
):
    micro, slots = images.shape[:2]
    every = micro * slots
    section = lax.axis_index("section")
    core = lax.axis_index("core")
    shards = lax.axis_size("chip") * lax.axis_size("core")
    index = lax.axis_index("chip") * lax.axis_size("core") + core
    is_first = section == 0

    packed = pack_weights(
        norm_gains, vectors, qkv_weight, proj_weight, hidden_weight, hidden_bias, out_weight, index, shards
    )
    gathered = lax.all_gather(packed, ("section", *SHARDED)).reshape(2, shards, *packed.shape)
    if shards == BLOCKS:
        weights = gathered
    else:
        weights = jnp.stack([merge_shards(gathered[layer], shards) for layer in range(2)])

    other_table = lax.ppermute(bias_table[0], "section", SWAP)
    bias0 = bias_arrays(jnp.where(is_first, bias_table[0], other_table), False)
    bias1 = bias_arrays(jnp.where(is_first, other_table, bias_table[0]), True)
    perms = permutations()
    perm0, perm1 = (jnp.asarray(mat, bf16) for mat in perms)
    perm0_t, perm1_t = (jnp.asarray(mat.T, bf16) for mat in perms)

    counts = live_counts[:, 0]
    other_counts = lax.ppermute(counts, "core", SWAP)
    counts = jnp.stack([jnp.where(core == 0, counts, other_counts), jnp.where(core == 0, other_counts, counts)])
    live = (jnp.arange(slots)[None, None, :] < counts[:, :, None]).reshape(-1)
    place = jnp.cumsum(live.astype(jnp.int32)) - 1
    total = jnp.sum(live.astype(jnp.int32))
    rank = 2 * core + section
    chip = lax.axis_index("chip")
    split_core = core if shards == BLOCKS else jnp.int32(0)
    count = (total - rank + 3) // 4
    wanted = jnp.minimum(jnp.arange(LIST), count - 1) * 4 + rank
    hits = live[None, :] & (place[None, :] == wanted[:, None])
    entry = jnp.arange(2 * every)
    entry = jnp.where(entry // every == core, entry % every, every + entry % every)
    mine = jnp.sum(jnp.where(hits, entry[None, :], 0), axis=1)
    where = jnp.concatenate([count[None], mine, jnp.full((1,), every), split_core[None], chip[None], section[None]]).astype(jnp.int32)
    live = lax.dynamic_slice(live, (core * every,), (every,))
    place = lax.dynamic_slice(place, (core * every,), (every,))
    kind = 2 * (place % 4 // 2 != core).astype(jnp.int32) + (place % 2 != section).astype(jnp.int32)
    flags = jnp.concatenate([jnp.where(live, kind, 4), jnp.maximum(place, 0) // 4]).astype(jnp.int32)
    other_images = lax.ppermute(images, "core", SWAP)
    other_out_grad = lax.ppermute(out_grad, "core", SWAP)

    def assemble(own, got, dtype):
        others = [lax.ppermute(rows, "core", SWAP) for rows in (own, got)]
        return run_spread(flags, [own, got, *others], micro, slots, dtype)

    rows0, *kept = run_first(where, images, other_images, weights, perm0, perm0_t, bias0)
    own_rows, sent_rows, grads1, packed1 = run_second(
        where, rows0, out_grad, other_out_grad, weights, perm1, perm1_t, bias1
    )
    got_rows = lax.ppermute(sent_rows, "section", SWAP)
    sums1 = lax.psum_scatter(split_shards(packed1, shards), SHARDED, scatter_dimension=0)
    own_grads, sent_grads, keep0, send0 = run_third(
        where, images, other_images, grads1, weights, perm0, perm0_t, kept
    )
    own_grads, sent_grads, keep0, send0, got_rows = lax.optimization_barrier(
        (own_grads, sent_grads, keep0, send0, got_rows)
    )
    if shards == BLOCKS:
        got0 = lax.ppermute(send0, "core", SWAP)
        blocks = run_add(chip, keep0, got0)
        blocks, sent_grads, own_grads, own_rows = lax.optimization_barrier(
            (blocks, sent_grads, own_grads, own_rows)
        )
        parts = [blocks[0]] + [shift(blocks[d], d) for d in range(1, len(blocks))]
    else:
        packed0 = jnp.stack([keep0, send0], axis=1).reshape(GRADS.shape)
        parts = [lax.psum_scatter(split_shards(packed0, shards), SHARDED, scatter_dimension=0)]
    got_grads = lax.ppermute(sent_grads, "section", SWAP)
    layer_out = assemble(own_rows, got_rows, bf16)
    parts, sums1, layer_out = lax.optimization_barrier((parts, sums1, layer_out))
    own_sums, sent_sums = run_parts(section, sums1, parts)
    got_sums = lax.ppermute(sent_sums, "section", SWAP)
    own_grads, own_sums = lax.optimization_barrier((own_grads, own_sums))
    input_out = assemble(own_grads, got_grads, f32)
    got_sums, input_out = lax.optimization_barrier((got_sums, input_out))
    finals = run_final(index, own_sums, got_sums, shards)
    return (
        layer_out.transpose(0, 2, 1, 3)[None],
        input_out.transpose(0, 2, 1, 3)[None],
        *[array[None] for array in finals],
    )


def solution(mesh):
    shape = (mesh.shape["section"], mesh.shape["fsdp"] // 2, 2)
    mesh = jax.sharding.Mesh(mesh.devices.reshape(shape), ("section", *SHARDED))
    in_specs = (
        P(None, SHARDED, None, None),
        P(None, SHARDED),
        P("section", None, SHARDED),
        P("section", None, SHARDED),
        P("section", SHARDED, None),
        P("section", SHARDED, None),
        P("section", SHARDED, None),
        P("section", SHARDED),
        P("section", SHARDED, None),
        P("section", None, None),
        P(None, SHARDED, None, None),
    )
    out_specs = (
        P("section", None, SHARDED, None, None),
        P("section", None, SHARDED, None, None),
        P("section", None, SHARDED),
        P("section", None, SHARDED),
        P("section", SHARDED, None),
        P("section", SHARDED, None),
        P("section", SHARDED, None),
        P("section", SHARDED),
        P("section", SHARDED, None),
        P("section", None, None),
    )
    return jax.shard_map(
        on_device, mesh=mesh, in_specs=in_specs, out_specs=out_specs, check_vma=False
    )
```

```python
import functools
import math

import jax
import jax.numpy as jnp
import numpy as np
from jax import lax
from jax.experimental import pallas as pl
from jax.experimental.pallas import tpu as pltpu
from jax.sharding import PartitionSpec as P

WIN = 7
GRID = 14
SHIFT = 3
TABLE = 169
HEADS = 16
HEAD = 32
D = 512
FF = 2048
TOK = 196
PAD = 208
PAIR = 2
BOTH = PAIR * PAD
WTOK = 64
WINS = 4
ALL = WINS * WTOK
GROUP = 4
GROUPS = HEADS // GROUP
CH = FF // D
BLOCKS = 16
ROWS = D // BLOCKS
QKV_AT, PROJ_AT, HID_AT, OUT_AT, SMALL_AT = 0, 96, 128, 256, 384
PACK_ROWS = 400
GRAD_ROWS = 416
EPS = 1e-05
LOG2E = 1.4426950408889634
SCALE = HEAD**-0.5
LOWEST = -1e30
LIST = 8
VMEM_LIMIT = 60 * 1024 * 1024
SHARDED = ("chip", "core")
SWAP = [(0, 1), (1, 0)]

bf16 = jnp.bfloat16
f32 = jnp.float32


def window_places():
    tables = []
    for shift in (0, SHIFT):
        table = np.full((ALL,), -1, np.int64)
        for window in range(WINS):
            for r in range(WIN):
                for c in range(WIN):
                    row = ((window // 2) * WIN + r + shift) % GRID
                    column = ((window % 2) * WIN + c + shift) % GRID
                    table[window * WTOK + 8 * r + c] = row * GRID + column
        tables.append(table)
    return tables


def permutations():
    mats = []
    for table in window_places():
        mat = np.zeros((ALL, PAD), np.float32)
        for at, token in enumerate(table):
            if token >= 0:
                mat[at, token] = 1.0
        mats.append(mat)
    return mats


def pair_offsets():
    place = np.arange(WTOK)
    r, c = place // 8, place % 8
    real = (r < WIN) & (c < WIN)
    offset = (r[None, :] - r[:, None] + WIN - 1) * (2 * WIN - 1) + c[None, :] - c[:, None] + WIN - 1
    return np.where(real[None, :] & real[:, None], offset, -1)


def region_masks():
    line = np.arange(GRID)
    band = (line >= GRID - WIN).astype(int) + (line >= GRID - SHIFT).astype(int)
    out = np.zeros((WINS, WTOK, WTOK), np.float32)
    for window in range(WINS):
        ids = np.full((WTOK,), -1)
        for r in range(WIN):
            for c in range(WIN):
                ids[8 * r + c] = (
                    3 * band[(window // 2) * WIN + r] + band[(window % 2) * WIN + c]
                )
        out[window] = np.where(ids[:, None] != ids[None, :], -100.0, 0.0)
    return out


def bias_arrays(table, masked):
    offsets = pair_offsets()
    pick = jnp.asarray(offsets.reshape(-1, 1), jnp.int32) == jnp.arange(TABLE, dtype=jnp.int32)[None, :]
    flat = jnp.dot(pick.astype(f32), table, precision=lax.Precision.HIGHEST)
    bias = flat.reshape(WTOK, WTOK, GROUPS, GROUP).transpose(2, 0, 3, 1)
    if masked:
        bias = bias[None] + jnp.asarray(region_masks())[:, None, :, None, :]
    else:
        bias = bias[None]
    place = np.arange(WTOK)
    real_key = (place // 8 < WIN) & (place % 8 < WIN)
    bias = jnp.where(jnp.asarray(real_key)[None, None, :, None, None], bias * LOG2E, LOWEST)
    return bias.reshape(bias.shape[0], GROUPS, WTOK, GROUP * WTOK)


def dot(a, b):
    return jnp.dot(a, b, preferred_element_type=f32)


def dot_nt(a, b):
    return lax.dot_general(a, b, (((1,), (1,)), ((), ())), preferred_element_type=f32)


def dot_tn(a, b):
    return lax.dot_general(a, b, (((0,), (0,)), ((), ())), preferred_element_type=f32)


def block(w_ref, at):
    return w_ref[:, pl.ds(at, ROWS), :].reshape(D, D)


def hidden_blocks(w_ref):
    return jnp.concatenate([block(w_ref, HID_AT + k * ROWS) for k in range(CH)], axis=1)


def qkv_blocks(w_ref):
    return jnp.concatenate([block(w_ref, QKV_AT + at * ROWS) for at in range(3)], axis=1)


def out_block(w_ref, k):
    return w_ref[pl.ds(k * (BLOCKS // CH), BLOCKS // CH), OUT_AT:SMALL_AT, :].reshape(D, D)


def normalize(values):
    center = values - jnp.mean(values, axis=-1, keepdims=True)
    inverse = lax.rsqrt(jnp.mean(center * center, axis=-1, keepdims=True) + EPS)
    return center * inverse, inverse


def norm_backward(grad_hat, hat, inverse):
    mean = jnp.mean(grad_hat, axis=-1, keepdims=True)
    along = jnp.mean(grad_hat * hat, axis=-1, keepdims=True)
    return inverse * (grad_hat - mean - hat * along)


ERF_T = 0.3275911
ERF_C = (0.254829592, -0.284496736, 1.421413741, -1.453152027, 1.061405429)


def gelu_and_slope(u):
    u = u.astype(bf16)
    size = jnp.abs(u)
    t = pltpu.reciprocal(size * bf16(ERF_T * 0.5**0.5) + bf16(1.0), approx=True)
    bell = jnp.exp2(u * u * bf16(-0.5 * LOG2E))
    tail = bf16(0.5 * ERF_C[4])
    for c in ERF_C[3::-1]:
        tail = tail * t + bf16(0.5 * c)
    tail = tail * t * bell
    phi = jnp.where(u >= bf16(0.0), bf16(1.0) - tail, tail)
    return jnp.maximum(u, bf16(0.0)) - size * tail, phi + u * bell * bf16((0.5 / math.pi) ** 0.5)


def head_masks():
    lane_head = lax.broadcasted_iota(jnp.int32, (WTOK, GROUP * HEAD), 1) // HEAD
    return [(lane_head == h).astype(f32).astype(bf16) for h in range(GROUP)]


def spread_heads(tile, masks):
    return jnp.concatenate([tile * mask for mask in masks], axis=0)


def put_diagonal(out_ref, image, group, pair, even, odd):
    for h in range(GROUP):
        rows, lanes = slice(h * HEAD, (h + 1) * HEAD), slice(h * WTOK, (h + 1) * WTOK)
        both = jnp.concatenate([even[rows, lanes], odd[rows, lanes]], axis=1)
        at = group * GROUP * HEAD + h * HEAD
        out_ref[image, at : at + HEAD, pair * 128 : (pair + 1) * 128] = both.astype(bf16)


def tiles_of(pair, group):
    lanes = slice(group * GROUP * HEAD, (group + 1) * GROUP * HEAD)
    for image in range(PAIR):
        for window in (2 * pair, 2 * pair + 1):
            at = image * ALL + window * WTOK
            yield image, window, slice(at, at + WTOK), lanes


def attention_forward(q_ref, k_ref, v_ref, p_ref, ot_ref, bias_ref):
    masks = head_masks()
    bias_windows = bias_ref.shape[0]

    def scores_of(tile):
        _, window, rows, lanes = tile
        scores = dot_nt(k_ref[rows, lanes], spread_heads(q_ref[rows, lanes], masks)) * (SCALE * LOG2E)
        return scores + bias_ref[window if bias_windows > 1 else 0, window_group]

    def probs_of(tile, scores):
        powers = jnp.exp2(scores - jnp.max(scores, axis=0, keepdims=True))
        probs = (powers * (1.0 / jnp.sum(powers, axis=0, keepdims=True))).astype(bf16)
        p_ref[tile[0], tile[1], window_group] = probs
        return probs

    def product_of(tile, probs):
        return dot_tn(v_ref[tile[2], tile[3]], probs)

    for pair in range(WINS // 2):
        for window_group in range(GROUPS):
            tiles = list(tiles_of(pair, window_group))
            for image in range(PAIR):
                two = tiles[2 * image : 2 * image + 2]
                products = [product_of(tile, probs_of(tile, scores_of(tile))) for tile in two]
                put_diagonal(ot_ref, image, window_group, pair, *products)


def attention_backward(q_ref, k_ref, v_ref, p_ref, do_ref, dqt_ref, dk_ref, dv_ref, score_ref):
    masks = head_masks()
    for pair in range(WINS // 2):
        for group in range(GROUPS):
            tiles = list(tiles_of(pair, group))

            def spread_of(ref, tile):
                return spread_heads(ref[tile[2], tile[3]], masks)

            def grads_of(tile, spread):
                prob = p_ref[tile[0], tile[1], group]
                grad_probs = dot_nt(v_ref[tile[2], tile[3]], spread)
                dv_ref[tile[2], tile[3]] = dot(prob, spread).astype(bf16)
                prob = prob.astype(f32)
                weighted = grad_probs * prob
                return weighted - prob * jnp.sum(weighted, axis=0, keepdims=True)

            def product_of(tile, low):
                dk_ref[tile[2], tile[3]] = (dot(low, spread_of(q_ref, tile)) * SCALE).astype(bf16)
                return dot_tn(k_ref[tile[2], tile[3]], low) * SCALE

            spreads = [spread_of(do_ref, tile) for tile in tiles]
            grads = [grads_of(tile, spread) for tile, spread in zip(tiles, spreads)]
            score_ref[group] += (grads[0] + grads[1]) + (grads[2] + grads[3])
            products = [product_of(tile, grad.astype(bf16)) for tile, grad in zip(tiles, grads)]
            for image in range(PAIR):
                put_diagonal(dqt_ref, image, group, pair, *products[2 * image : 2 * image + 2])


def to_windows(perm_ref, rows):
    return jnp.concatenate(
        [dot(perm_ref[...], rows[i * PAD : (i + 1) * PAD]).astype(bf16) for i in range(PAIR)], axis=0
    )


def from_windows(perm_t_ref, ref):
    return jnp.concatenate(
        [dot(perm_t_ref[...], ref[i * ALL : (i + 1) * ALL, :]) for i in range(PAIR)], axis=0
    )


def from_windows_turned(perm_t_ref, ref):
    return jnp.concatenate([dot_nt(perm_t_ref[...], ref[i]) for i in range(PAIR)], axis=0)


def forward_part(x_ref, w_ref, small_ref, perm_ref, perm_t_ref, bias_ref, a):
    hat1, inv1 = normalize(x_ref[...])
    norm1 = (hat1 * small_ref[0:1, :] + small_ref[2:3, :]).astype(bf16)
    blocks = to_windows(perm_ref, norm1)
    a["q"][...] = (dot(blocks, block(w_ref, QKV_AT)) + small_ref[3:4, :]).astype(bf16)
    a["k"][...] = dot(blocks, block(w_ref, QKV_AT + ROWS)).astype(bf16)
    a["v"][...] = (dot(blocks, block(w_ref, QKV_AT + 2 * ROWS)) + small_ref[4:5, :]).astype(bf16)
    attention_forward(a["q"], a["k"], a["v"], a["p"], a["ot"], bias_ref)
    mixed = from_windows_turned(perm_t_ref, a["ot"]).astype(bf16)
    resid = x_ref[...] + dot(mixed, block(w_ref, PROJ_AT)) + small_ref[5:6, :]
    a["resid"][...] = resid
    hat2, inv2 = normalize(resid)
    norm2 = (hat2 * small_ref[1:2, :] + small_ref[6:7, :]).astype(bf16)
    a["n2"][...] = norm2
    for k in range(CH):
        lanes = slice(k * D, (k + 1) * D)
        hidden = dot(norm2, block(w_ref, HID_AT + k * ROWS)) + small_ref[8 + k : 9 + k, :]
        a["g"][:, lanes], a["slope"][:, lanes] = gelu_and_slope(hidden)
    out_weight = w_ref[:, OUT_AT:SMALL_AT, :].reshape(FF, D)
    a["h"][...] = resid + small_ref[7:8, :] + dot(a["g"][...], out_weight)
    return hat1, inv1, norm1, hat2, inv2


def add_rows(ref, at, values):
    ref[at] += jnp.sum(values.reshape(BOTH // 8, 8, D), axis=0)


def backward_part(e_ref, hats, w_ref, small_ref, perm_ref, perm_t_ref, a, b):
    hat1, inv1, norm1, hat2, inv2 = hats

    out_grad = e_ref[...].astype(bf16)
    add_rows(b["rows"], 7, out_grad.astype(f32))
    b["dz"][...] = out_grad
    b["dzt"][...] = out_grad.T
    b["n2t"][...] = a["n2"][...].T
    for k in range(CH):
        lanes = slice(k * D, (k + 1) * D)
        grad_hidden = dot_nt(b["dz"][...], out_block(w_ref, k)) * a["slope"][:, lanes].astype(f32)
        add_rows(b["rows"], 8 + k, grad_hidden)
        low = grad_hidden.astype(bf16)
        b["du"][:, lanes] = low
        at = HID_AT + k * ROWS
        b["acc"][:, at : at + ROWS, :] += dot(b["n2t"][...], low).reshape(BLOCKS, ROWS, D)
        b["acc_out"][k] += dot(b["dzt"][...], a["g"][:, lanes])
    dn2 = dot_nt(b["du"][...], hidden_blocks(w_ref))
    add_rows(b["rows"], 1, dn2 * hat2)
    add_rows(b["rows"], 6, dn2)
    dr = e_ref[...] + norm_backward(dn2 * small_ref[1:2, :], hat2, inv2)
    low = dr.astype(bf16)
    add_rows(b["rows"], 5, low.astype(f32))
    attn = to_windows(perm_ref, low)
    b["do"][...] = dot_nt(attn, block(w_ref, PROJ_AT)).astype(bf16)
    proj = dot(a["ot"][0], attn[:ALL]) + dot(a["ot"][1], attn[ALL:])
    b["acc"][:, PROJ_AT : PROJ_AT + ROWS, :] += proj.reshape(BLOCKS, ROWS, D)
    attention_backward(
        a["q"], a["k"], a["v"], a["p"], b["do"], b["dqt"], b["dk"], b["dv"], b["scores"]
    )
    norm1_t = norm1.T
    grad_qkv = []
    for at in range(3):
        if at == 0:
            rows = from_windows_turned(perm_t_ref, b["dqt"])
        else:
            rows = from_windows(perm_t_ref, b["dk" if at == 1 else "dv"])
        if at != 1:
            add_rows(b["rows"], 3 + at // 2, rows)
        rows = rows.astype(bf16)
        grad_qkv.append(rows)
        take = slice(QKV_AT + at * ROWS, QKV_AT + (at + 1) * ROWS)
        b["acc"][:, take, :] += dot(norm1_t, rows).reshape(BLOCKS, ROWS, D)
    dn1 = dot_nt(jnp.concatenate(grad_qkv, axis=1), qkv_blocks(w_ref))
    add_rows(b["rows"], 0, dn1 * hat1)
    add_rows(b["rows"], 2, dn1)
    return dr + norm_backward(dn1 * small_ref[0:1, :], hat1, inv1)


def clear_sums(b):
    for name in ("acc", "acc_out", "rows", "scores"):
        b[name][...] = jnp.zeros(b[name].shape, f32)


def table_rows(score_ref, fold_ref):
    lane = lax.broadcasted_iota(jnp.int32, (WTOK, 128), 1)
    for head in range(HEADS):
        group, h = head // GROUP, head % GROUP
        tile = score_ref[group, :, 128 * (h // 2) : 128 * (h // 2) + 128]
        if h % 2:
            tile = pltpu.roll(tile, WTOK, 1)
        tile = jnp.where(lane < WTOK, tile, 0.0)
        total = jnp.zeros((8, 128), f32)
        for r in range(WIN):
            turned = tile[8 * r : 8 * r + 8]
            if r < WIN - 1:
                turned = pltpu.roll(turned, 8 * (WIN - 1 - r), 1)
            total = total + turned
        fold_ref[8 * head : 8 * head + 8, :] = total
    lane = lax.broadcasted_iota(jnp.int32, (128, 256), 0)
    goal = lax.broadcasted_iota(jnp.int32, (128, 256), 1)
    out = jnp.zeros((HEADS, 256), f32)
    for c in range(WIN):
        pick = (goal == 16 * (lane // 8) + lane % 8 - c + WIN - 1) & (lane % 8 < WIN)
        out = out + jnp.dot(
            fold_ref[pl.ds(c, HEADS, stride=8), :],
            pick.astype(f32),
            precision=lax.Precision.HIGHEST,
            preferred_element_type=f32,
        )
    return out


def write_sums(b, fold_ref, put):
    everything = slice(0, D)
    width = FF // BLOCKS
    for owner in range(BLOCKS):
        k, lane = owner // (BLOCKS // CH), width * (owner % (BLOCKS // CH))
        put(owner, slice(0, OUT_AT), everything, lambda: b["acc"][owner].astype(bf16))
        for at in range(D // width):
            lanes = slice(at * width, (at + 1) * width)
            put(
                owner,
                slice(OUT_AT, SMALL_AT),
                lanes,
                lambda: b["acc_out"][k, lanes, lane : lane + width].astype(bf16),
            )
    rows = jnp.sum(b["rows"][...], axis=1)
    rows = jnp.concatenate([rows, jnp.zeros((4, D), f32)], axis=0).astype(bf16)
    table = table_rows(b["scores"], fold_ref)
    table = jnp.concatenate([table, jnp.zeros((HEADS, D - 256), f32)], axis=1).astype(bf16)
    for owner in range(BLOCKS):
        put(owner, slice(SMALL_AT, PACK_ROWS), everything, lambda: rows)
        put(owner, slice(PACK_ROWS, GRAD_ROWS), everything, lambda: table)


def sum_small(w_ref, small_ref):
    small_ref[...] = jnp.sum(w_ref[:, SMALL_AT:PACK_ROWS, :].astype(f32), axis=0)


KEPT = {
    "q": ((PAIR * ALL, D), bf16),
    "k": ((PAIR * ALL, D), bf16),
    "v": ((PAIR * ALL, D), bf16),
    "p": ((PAIR, WINS, GROUPS, WTOK, GROUP * WTOK), bf16),
    "ot": ((PAIR, D, ALL), bf16),
    "resid": ((BOTH, D), f32),
    "g": ((BOTH, FF), bf16),
    "slope": ((BOTH, FF), bf16),
}
LOCAL_F = {"n2": ((BOTH, D), bf16), "h": ((BOTH, D), f32)}
LOCAL_B = {
    "acc": ((BLOCKS, OUT_AT, D), f32),
    "acc_out": ((CH, D, D), f32),
    "rows": ((12, 8, D), f32),
    "scores": ((GROUPS, WTOK, GROUP * WTOK), f32),
    "dz": ((BOTH, D), bf16),
    "dzt": ((D, BOTH), bf16),
    "n2t": ((D, BOTH), bf16),
    "du": ((BOTH, FF), bf16),
    "do": ((PAIR * ALL, D), bf16),
    "dqt": ((PAIR, D, ALL), bf16),
    "dk": ((PAIR * ALL, D), bf16),
    "dv": ((PAIR * ALL, D), bf16),
}


def scratch(shapes):
    return [pltpu.VMEM(shape, dtype) for shape, dtype in shapes.values()]


def load_images(goal_ref, where_ref, step, refs):
    for image in range(PAIR):
        at = PAIR * step + image
        rows = slice(image * PAD, image * PAD + TOK)
        for core in range(2):

            @pl.when((at < where_ref[0]) & (where_ref[1 + at] // where_ref[1 + LIST] == core))
            def _():
                goal_ref[rows, :] = refs[2 * image + core][0, 0].astype(f32)

        @pl.when(at >= where_ref[0])
        def _():
            goal_ref[rows, :] = jnp.zeros((TOK, D), f32)


def load_rows(goal_ref, ref):
    for image in range(PAIR):
        goal_ref[image * PAD : image * PAD + TOK, :] = ref[image, 0:TOK, :].astype(f32)


def store_sides(own_ref, send_ref, where_ref, first, second):
    for section in range(2):

        @pl.when(where_ref[4 + LIST] == section)
        def _():
            own_ref[...] = second if section else first
            send_ref[...] = first if section else second


def store_rows(ref, values):
    for image in range(PAIR):
        ref[image] = values[image * PAD : (image + 1) * PAD].astype(bf16)


def first_kernel(where_ref, x0, x1, x2, x3, w_ref, perm_ref, perm_t_ref, bias_ref, h_ref, *refs):
    kept = dict(zip(KEPT, refs))
    refs = refs[len(KEPT) :]
    kept.update(zip(LOCAL_F, refs))
    xs_ref, small_ref = refs[len(LOCAL_F) :]
    kept = {name: (ref.at[0] if name in KEPT else ref) for name, ref in kept.items()}
    step = pl.program_id(0)

    @pl.when(step == 0)
    def _():
        xs_ref[...] = jnp.zeros(xs_ref.shape, f32)
        sum_small(w_ref, small_ref)

    @pl.when(PAIR * step < where_ref[0])
    def _():
        load_images(xs_ref, where_ref, step, (x0, x1, x2, x3))
        forward_part(xs_ref, w_ref, small_ref, perm_ref, perm_t_ref, bias_ref, kept)
        store_rows(h_ref, kept["h"][...])


def second_kernel(
    where_ref,
    x_ref,
    e0,
    e1,
    e2,
    e3,
    w_ref,
    perm_ref,
    perm_t_ref,
    bias_ref,
    own_ref,
    send_ref,
    ig_ref,
    gp_ref,
    *refs,
):
    names = {**KEPT, **LOCAL_F}
    kept = dict(zip(names, refs))
    refs = refs[len(names) :]
    sums = dict(zip(LOCAL_B, refs))
    xs_ref, es_ref, small_ref, fold_ref = refs[len(LOCAL_B) :]
    step = pl.program_id(0)

    @pl.when(step == 0)
    def _():
        xs_ref[...] = jnp.zeros(xs_ref.shape, f32)
        es_ref[...] = jnp.zeros(es_ref.shape, f32)
        sum_small(w_ref, small_ref)
        clear_sums(sums)

    @pl.when(PAIR * step < where_ref[0])
    def _():
        load_rows(xs_ref, x_ref)
        load_images(es_ref, where_ref, step, (e0, e1, e2, e3))
        hats = forward_part(xs_ref, w_ref, small_ref, perm_ref, perm_t_ref, bias_ref, kept)
        out = kept["h"][...].reshape(PAIR, PAD, D).astype(bf16)
        store_sides(own_ref, send_ref, where_ref, x_ref[...], out)
        grad = backward_part(es_ref, hats, w_ref, small_ref, perm_ref, perm_t_ref, kept, sums)
        store_rows(ig_ref, grad)

    @pl.when(step == pl.num_programs(0) - 1)
    def _():
        def put(owner, rows, lanes, values):
            gp_ref[owner, rows, lanes] = values()

        write_sums(sums, fold_ref, put)


def third_kernel(where_ref, x0, x1, x2, x3, e_ref, w_ref, perm_ref, perm_t_ref, *refs):
    kept = {name: ref.at[0] for name, ref in zip(KEPT, refs)}
    own_ref, other_ref, keep_ref, send_ref = refs[len(KEPT) : len(KEPT) + 4]
    refs = refs[len(KEPT) + 4 :]
    sums = dict(zip(LOCAL_B, refs))
    n2_ref, xs_ref, es_ref, small_ref, fold_ref = refs[len(LOCAL_B) :]
    kept["n2"] = n2_ref
    step = pl.program_id(0)

    @pl.when(step == 0)
    def _():
        xs_ref[...] = jnp.zeros(xs_ref.shape, f32)
        es_ref[...] = jnp.zeros(es_ref.shape, f32)
        sum_small(w_ref, small_ref)
        clear_sums(sums)

    @pl.when(PAIR * step < where_ref[0])
    def _():
        load_images(xs_ref, where_ref, step, (x0, x1, x2, x3))
        load_rows(es_ref, e_ref)
        hat1, inv1 = normalize(xs_ref[...])
        norm1 = (hat1 * small_ref[0:1, :] + small_ref[2:3, :]).astype(bf16)
        hat2, inv2 = normalize(kept["resid"][...])
        n2_ref[...] = (hat2 * small_ref[1:2, :] + small_ref[6:7, :]).astype(bf16)
        hats = (hat1, inv1, norm1, hat2, inv2)
        grad = backward_part(es_ref, hats, w_ref, small_ref, perm_ref, perm_t_ref, kept, sums)
        out = grad.reshape(PAIR, PAD, D).astype(bf16)
        store_sides(own_ref, other_ref, where_ref, out, e_ref[...])

    @pl.when(step == pl.num_programs(0) - 1)
    def _():
        for core in range(2):

            @pl.when(where_ref[2 + LIST] == core)
            def _():
                def put(owner, rows, lanes, values):
                    goal_ref = keep_ref if owner % 2 == core else send_ref
                    goal_ref[owner // 2, rows, lanes] = values()

                write_sums(sums, fold_ref, put)


def spread_kernel(flags_ref, *refs):
    out_ref, held_ref = refs[-2:]
    slots = out_ref.shape[2]
    for slot in range(slots):
        kind = flags_ref[pl.program_id(0) * slots + slot]
        for at in range(4):

            @pl.when(kind == at)
            def _():
                held_ref[slot] = refs[4 * slot + at][0]

        @pl.when(kind == 4)
        def _():
            held_ref[slot] = jnp.zeros(held_ref.shape[1:], held_ref.dtype)

    values = [held_ref[slot, 0:TOK, :].astype(out_ref.dtype) for slot in range(slots)]
    if out_ref.dtype == f32:
        for slot in range(slots):
            out_ref[0, :, slot, :] = values[slot]
    else:
        out_ref[0] = jnp.stack(values, axis=1)


def whole(array):
    zeros = (0,) * array.ndim
    return pl.BlockSpec(array.shape, lambda *_: zeros, pipeline_mode=pl.Buffered(1))


def of_layer(weights, layer):
    return pl.BlockSpec(
        (None, *weights.shape[1:]), lambda *_: (layer, 0, 0, 0), pipeline_mode=pl.Buffered(1)
    )


def params():
    return pltpu.CompilerParams(vmem_limit_bytes=VMEM_LIMIT, dimension_semantics=("arbitrary",))


def cost(images, layers):
    return pl.CostEstimate(
        flops=int(images * layers * 1.6e9), bytes_accessed=int(images * 4e6), transcendentals=int(images * 1e6)
    )


def live_step(k, where):
    return jnp.minimum(k, (where[0] - 1) // PAIR)


def by_step(shape):
    zeros = (0,) * len(shape)
    return pl.BlockSpec((1, *shape), lambda k, where: (live_step(k, where), *zeros))


def by_pair():
    return pl.BlockSpec((PAIR, PAD, D), lambda k, where: (live_step(k, where), 0, 0))


def by_image(micro, slots):
    def spec(image, core):
        def at(k, where):
            found = jnp.int32(0)
            for earlier in range(LIST // PAIR):
                entry = where[1 + PAIR * earlier + image]
                use = (earlier <= k) & (entry // (micro * slots) == core)
                found = jnp.where(use, entry % (micro * slots), found)
            return (found // slots, found % slots, 0, 0)

        return pl.BlockSpec((1, 1, TOK, D), at)

    return [spec(image, core) for image in range(PAIR) for core in range(2)]


def run_first(where, images, others, weights, perm, perm_t, bias):
    steps = LIST // PAIR
    outs = list(KEPT.values())
    return pl.pallas_call(
        first_kernel,
        grid_spec=pltpu.PrefetchScalarGridSpec(
            num_scalar_prefetch=1,
            grid=(steps,),
            in_specs=by_image(*images.shape[:2])
            + [of_layer(weights, 0)]
            + [whole(array) for array in (perm, perm_t, bias)],
            out_specs=[by_pair()] + [by_step(shape) for shape, _ in outs],
            scratch_shapes=scratch(LOCAL_F) + [pltpu.VMEM((BOTH, D), f32), pltpu.VMEM((16, D), f32)],
        ),
        out_shape=[IMAGES]
        + [jax.ShapeDtypeStruct((steps, *shape), dtype) for shape, dtype in outs],
        compiler_params=params(),
        cost_estimate=cost(LIST, 1),
        name="layer0_forward",
    )(where, images, others, images, others, weights, perm, perm_t, bias)


IMAGES = jax.ShapeDtypeStruct((LIST, PAD, D), bf16)
GRADS = jax.ShapeDtypeStruct((BLOCKS, GRAD_ROWS, D), bf16)
HALF = jax.ShapeDtypeStruct((BLOCKS // 2, GRAD_ROWS, D), bf16)


def run_second(where, rows, out_grad, others, weights, perm, perm_t, bias):
    return pl.pallas_call(
        second_kernel,
        grid_spec=pltpu.PrefetchScalarGridSpec(
            num_scalar_prefetch=1,
            grid=(LIST // PAIR,),
            in_specs=[by_pair()]
            + by_image(*out_grad.shape[:2])
            + [of_layer(weights, 1)]
            + [whole(array) for array in (perm, perm_t, bias)],
            out_specs=[by_pair(), by_pair(), by_pair(), whole(GRADS)],
            scratch_shapes=scratch({**KEPT, **LOCAL_F})
            + scratch(LOCAL_B)
            + [
                pltpu.VMEM((BOTH, D), f32),
                pltpu.VMEM((BOTH, D), f32),
                pltpu.VMEM((16, D), f32),
                pltpu.VMEM((128, 128), f32),
            ],
        ),
        out_shape=[IMAGES, IMAGES, IMAGES, GRADS],
        compiler_params=params(),
        cost_estimate=cost(LIST, 3),
        name="layer1_both",
    )(where, rows, out_grad, others, out_grad, others, weights, perm, perm_t, bias)


def run_third(where, images, others, grads, weights, perm, perm_t, kept):
    return pl.pallas_call(
        third_kernel,
        grid_spec=pltpu.PrefetchScalarGridSpec(
            num_scalar_prefetch=1,
            grid=(LIST // PAIR,),
            in_specs=by_image(*images.shape[:2])
            + [by_pair(), of_layer(weights, 0), whole(perm), whole(perm_t)]
            + [by_step(shape) for shape, _ in KEPT.values()],
            out_specs=[by_pair(), by_pair(), whole(HALF), whole(HALF)],
            scratch_shapes=scratch(LOCAL_B)
            + [
                pltpu.VMEM((BOTH, D), bf16),
                pltpu.VMEM((BOTH, D), f32),
                pltpu.VMEM((BOTH, D), f32),
                pltpu.VMEM((16, D), f32),
                pltpu.VMEM((128, 128), f32),
            ],
        ),
        out_shape=[IMAGES, IMAGES, HALF, HALF],
        compiler_params=params(),
        cost_estimate=cost(LIST, 2),
        name="layer0_backward",
    )(where, images, others, images, others, grads, weights, perm, perm_t, *kept)


def run_spread(flags, lists, micro, slots, dtype):
    def spec(slot, kind):
        def at(m, flags):
            i = m * slots + slot
            return (jnp.where(flags[i] == kind, flags[micro * slots + i], 0), 0, 0)

        return pl.BlockSpec((1, PAD, D), at)

    return pl.pallas_call(
        spread_kernel,
        grid_spec=pltpu.PrefetchScalarGridSpec(
            num_scalar_prefetch=1,
            grid=(micro,),
            in_specs=[spec(slot, kind) for slot in range(slots) for kind in range(4)],
            out_specs=pl.BlockSpec((1, TOK, slots, D), lambda m, flags: (m, 0, 0, 0)),
            scratch_shapes=[pltpu.VMEM((slots, PAD, D), bf16)],
        ),
        out_shape=jax.ShapeDtypeStruct((micro, TOK, slots, D), dtype),
        compiler_params=params(),
        name="spread_images",
    )(flags, *(list(lists) * slots))


PART = GRAD_ROWS // 2


def add_cores_kernel(section_ref, mine_ref, got_ref, keep_ref, send_ref):
    for section in range(2):

        @pl.when(section_ref[0] == section)
        def _():
            for at in range(mine_ref.shape[0]):
                for half, ref in ((section, keep_ref), (1 - section, send_ref)):
                    rows = slice(half * PART, (half + 1) * PART)
                    total = mine_ref[at, rows, :].astype(f32) + got_ref[at, rows, :].astype(f32)
                    ref[at] = total.astype(bf16)


def add_sections_kernel(chip_ref, keep_ref, got_ref, *out_refs):
    for d, out_ref in enumerate(out_refs):
        at = chip_ref[0] ^ d
        out_ref[...] = (keep_ref[at].astype(f32) + got_ref[at].astype(f32)).astype(bf16)


def run_add(kernel, scalar, mine, got, outs, name):
    in_vmem = pl.BlockSpec(memory_space=pltpu.VMEM)
    return pl.pallas_call(
        kernel,
        grid_spec=pltpu.PrefetchScalarGridSpec(
            num_scalar_prefetch=1,
            grid=(),
            in_specs=[in_vmem] * 2,
            out_specs=[in_vmem] * len(outs),
        ),
        out_shape=outs,
        compiler_params=pltpu.CompilerParams(vmem_limit_bytes=VMEM_LIMIT),
        name=name,
    )(scalar.reshape(1).astype(jnp.int32), mine, got)


def parts_kernel(section_ref, first_ref, *refs):
    own_ref, send_ref = refs[-2:]
    total = refs[0][...].astype(f32)
    for ref in refs[1:-2]:
        total = total + ref[...].astype(f32)
    total = total.astype(bf16)
    halves = total.shape[0] < first_ref.shape[0]
    for section in range(2):
        total_ref, other_ref = (send_ref, own_ref) if section else (own_ref, send_ref)

        @pl.when(section_ref[0] == section)
        def _():
            other_ref[...] = first_ref[...]
            if halves:
                total_ref[section * PART : (section + 1) * PART, :] = total
                total_ref[(1 - section) * PART : (2 - section) * PART, :] = jnp.zeros((PART, D), bf16)
            else:
                total_ref[...] = total


def run_parts(section, sums1, parts):
    one = jax.ShapeDtypeStruct(sums1.shape, bf16)
    in_vmem = pl.BlockSpec(memory_space=pltpu.VMEM)
    return pl.pallas_call(
        parts_kernel,
        grid_spec=pltpu.PrefetchScalarGridSpec(
            num_scalar_prefetch=1,
            grid=(),
            in_specs=[in_vmem] * (1 + len(parts)),
            out_specs=[in_vmem] * 2,
        ),
        out_shape=[one] * 2,
        compiler_params=pltpu.CompilerParams(vmem_limit_bytes=VMEM_LIMIT),
        name="add_chips",
    )(section.reshape(1).astype(jnp.int32), sums1, *parts)


def final_kernel(place_ref, *refs):
    own_ref, got_ref, *out_refs, total_ref = refs
    gains_ref, vectors_ref, qkv_ref, proj_ref, hidden_ref, bias_ref, out_ref, table_ref = out_refs
    total_ref[...] = own_ref[...].astype(f32) + got_ref[...].astype(f32)
    index = place_ref[0]
    rows, width = qkv_ref.shape[0], out_ref.shape[0]
    for at in range(3):
        qkv_ref[:, at * D : (at + 1) * D] = total_ref[at * rows : (at + 1) * rows, :]
    proj_ref[...] = total_ref[3 * rows : 4 * rows, :]
    for at in range(CH):
        hidden_ref[:, at * D : (at + 1) * D] = total_ref[(4 + at) * rows : (5 + at) * rows, :]
    if width == FF // BLOCKS:
        for at in range(D // width):
            lanes = slice(at * width, (at + 1) * width)
            out_ref[:, lanes] = total_ref[8 * rows : 8 * rows + width, lanes].T
    else:
        out_ref[...] = total_ref[8 * rows : 8 * rows + width, :]
    small = total_ref[8 * rows + width : 8 * rows + width + 16, :]
    own = pltpu.roll(small, D - index * rows, 1)
    gains_ref[...] = own[0:2, :rows]
    for at in range(6):
        vectors_ref[at] = own[2 + at : 3 + at, :rows]
    row = lax.broadcasted_iota(jnp.int32, (16, D), 0)
    mine = jnp.where(row == 8 + index * width // D, small, 0.0)
    mine = jnp.sum(mine, axis=0, keepdims=True)
    mine = pltpu.roll(jnp.broadcast_to(mine, (8, D)), D - lax.rem(index * width, D), 1)
    bias_ref[...] = mine[0:1, :width]
    side = 2 * WIN - 1
    goal = lax.broadcasted_iota(jnp.int32, (TABLE, 256), 0)
    lane = lax.broadcasted_iota(jnp.int32, (TABLE, 256), 1)
    pick = (lane == 16 * (goal // side) + lax.rem(goal, side)).astype(f32)
    table = total_ref[8 * rows + width + 16 : 8 * rows + width + 32, 0:256]
    table_ref[...] = lax.dot_general(
        table,
        pick,
        (((1,), (1,)), ((), ())),
        precision=lax.Precision.HIGHEST,
        preferred_element_type=f32,
    )


def run_final(index, own, got, shards):
    rows, width = D // shards, FF // shards
    shapes = [
        (2, rows), (6, 1, rows), (rows, 3 * D), (rows, D), (rows, FF), (1, width), (width, D), (HEADS, TABLE)
    ]
    outs = pl.pallas_call(
        final_kernel,
        grid_spec=pltpu.PrefetchScalarGridSpec(
            num_scalar_prefetch=1,
            grid=(),
            in_specs=[pl.BlockSpec(memory_space=pltpu.VMEM)] * 2,
            out_specs=[pl.BlockSpec(memory_space=pltpu.VMEM)] * 8,
            scratch_shapes=[pltpu.VMEM(own.shape, f32)],
        ),
        out_shape=[jax.ShapeDtypeStruct(shape, f32) for shape in shapes],
        name="final_sums",
    )(index.reshape(1).astype(jnp.int32), own, got)
    outs = list(outs)
    outs[1] = outs[1].reshape(6, rows)
    outs[5] = outs[5].reshape(width)
    outs[7] = outs[7].T
    return outs


def pack_kernel(qkv_ref, proj_ref, hidden_ref, out_ref, small_ref, packed_ref):
    rows = qkv_ref.shape[0]
    for at in range(3):
        packed_ref[at * rows : (at + 1) * rows, :] = qkv_ref[:, at * D : (at + 1) * D]
    packed_ref[3 * rows : 4 * rows, :] = proj_ref[...]
    for at in range(CH):
        packed_ref[(4 + at) * rows : (5 + at) * rows, :] = hidden_ref[:, at * D : (at + 1) * D]
    width = out_ref.shape[0]
    packed_ref[8 * rows : 8 * rows + width, :] = out_ref[...]
    packed_ref[8 * rows + width : 8 * rows + width + 16, :] = small_ref[...]


def pack_weights(norm_gains, vectors, qkv, proj, hidden, hidden_bias, out, index, shards):
    small = jnp.concatenate([norm_gains[0], vectors[0]], axis=0)
    mine = jnp.arange(shards)[None, :, None] == index
    small = jnp.where(mine, small[:, None, :], jnp.zeros((), bf16)).reshape(8, D)
    bias = jnp.where(mine[0], hidden_bias, jnp.zeros((), bf16)).reshape(CH, D)
    small = jnp.concatenate([small, bias, jnp.zeros((4, D), bf16)], axis=0)
    rows = 8 * qkv.shape[1] + out.shape[1] + 16
    return pl.pallas_call(
        pack_kernel, out_shape=jax.ShapeDtypeStruct((rows, D), bf16), name="pack_weights"
    )(qkv[0], proj[0], hidden[0], out[0], small)


def regroup(array, rows_from, rows_to, goal):
    pieces, at = [], 0
    for rows, new_rows in zip(rows_from, rows_to):
        pieces.append(array[:, at : at + rows].reshape(goal, new_rows, D))
        at += rows
    return pieces


def merge_shards(gathered, shards):
    rows = D // shards
    parts = [rows] * 8 + [FF // shards]
    goals = [ROWS] * 8 + [FF // BLOCKS]
    pieces = regroup(gathered[:, : sum(parts)], parts, goals, BLOCKS)
    small = jnp.sum(gathered[:, sum(parts) :].astype(f32), axis=0).astype(bf16)
    small = jnp.where(jnp.arange(BLOCKS)[:, None, None] == 0, small[None], jnp.zeros((), bf16))
    return jnp.concatenate(pieces + [small], axis=1)


def exchange(array, d):
    chips = lax.axis_size("chip")
    return lax.ppermute(array, "chip", [(i, i ^ d) for i in range(chips)])


def split_shards(packed, shards):
    if shards == BLOCKS:
        return packed
    rows, width = D // shards, FF // BLOCKS
    parts = [ROWS] * 8 + [width]
    goals = [rows] * 8 + [FF // shards]
    turned = packed[:, OUT_AT:SMALL_AT].reshape(BLOCKS, width, D // width, width)
    turned = turned.transpose(0, 3, 2, 1).reshape(BLOCKS, width, D)
    blocks = jnp.concatenate([packed[:, :OUT_AT], turned], axis=1)
    pieces = regroup(blocks, parts, goals, shards)
    small = jnp.broadcast_to(packed[:1, SMALL_AT:], (shards, GRAD_ROWS - SMALL_AT, D))
    return jnp.concatenate(pieces + [small], axis=1)


def on_device(
    images,
    live_counts,
    norm_gains,
    vectors,
    qkv_weight,
    proj_weight,
    hidden_weight,
    hidden_bias,
    out_weight,
    bias_table,
    out_grad,
):
    micro, slots = images.shape[:2]
    every = micro * slots
    section = lax.axis_index("section")
    core = lax.axis_index("core")
    shards = lax.axis_size("chip") * lax.axis_size("core")
    index = lax.axis_index("chip") * lax.axis_size("core") + core
    is_first = section == 0

    packed = pack_weights(
        norm_gains, vectors, qkv_weight, proj_weight, hidden_weight, hidden_bias, out_weight, index, shards
    )
    gathered = lax.all_gather(packed, ("section", *SHARDED)).reshape(2, shards, *packed.shape)
    if shards == BLOCKS:
        weights = gathered
    else:
        weights = jnp.stack([merge_shards(gathered[layer], shards) for layer in range(2)])

    other_table = lax.ppermute(bias_table[0], "section", SWAP)
    bias0 = bias_arrays(jnp.where(is_first, bias_table[0], other_table), False)
    bias1 = bias_arrays(jnp.where(is_first, other_table, bias_table[0]), True)
    perms = permutations()
    perm0, perm1 = (jnp.asarray(mat, bf16) for mat in perms)
    perm0_t, perm1_t = (jnp.asarray(mat.T, bf16) for mat in perms)

    counts = live_counts[:, 0]
    other_counts = lax.ppermute(counts, "core", SWAP)
    counts = jnp.stack([jnp.where(core == 0, counts, other_counts), jnp.where(core == 0, other_counts, counts)])
    live = (jnp.arange(slots)[None, None, :] < counts[:, :, None]).reshape(-1)
    place = jnp.cumsum(live.astype(jnp.int32)) - 1
    total = jnp.sum(live.astype(jnp.int32))
    rank = 2 * core + section
    chip = lax.axis_index("chip")
    split_core = core if shards == BLOCKS else jnp.int32(0)
    count = (total - rank + 3) // 4
    wanted = jnp.minimum(jnp.arange(LIST), count - 1) * 4 + rank
    hits = live[None, :] & (place[None, :] == wanted[:, None])
    entry = jnp.arange(2 * every)
    entry = jnp.where(entry // every == core, entry % every, every + entry % every)
    mine = jnp.sum(jnp.where(hits, entry[None, :], 0), axis=1)
    where = jnp.concatenate([count[None], mine, jnp.full((1,), every), split_core[None], chip[None], section[None]]).astype(jnp.int32)
    live = lax.dynamic_slice(live, (core * every,), (every,))
    place = lax.dynamic_slice(place, (core * every,), (every,))
    kind = 2 * (place % 4 // 2 != core).astype(jnp.int32) + (place % 2 != section).astype(jnp.int32)
    flags = jnp.concatenate([jnp.where(live, kind, 4), jnp.maximum(place, 0) // 4]).astype(jnp.int32)
    other_images = lax.ppermute(images, "core", SWAP)
    other_out_grad = lax.ppermute(out_grad, "core", SWAP)

    def assemble(own, got, dtype):
        others = [lax.ppermute(rows, "core", SWAP) for rows in (own, got)]
        return run_spread(flags, [own, got, *others], micro, slots, dtype)

    rows0, *kept = run_first(where, images, other_images, weights, perm0, perm0_t, bias0)
    own_rows, sent_rows, grads1, packed1 = run_second(
        where, rows0, out_grad, other_out_grad, weights, perm1, perm1_t, bias1
    )
    got_rows = lax.ppermute(sent_rows, "section", SWAP)
    sums1 = lax.psum_scatter(split_shards(packed1, shards), SHARDED, scatter_dimension=0)
    own_grads, sent_grads, keep0, send0 = run_third(
        where, images, other_images, grads1, weights, perm0, perm0_t, kept
    )
    own_grads, sent_grads, keep0, send0, got_rows = lax.optimization_barrier(
        (own_grads, sent_grads, keep0, send0, got_rows)
    )
    if shards == BLOCKS:
        got0 = lax.ppermute(send0, "core", SWAP)
        half = jax.ShapeDtypeStruct((BLOCKS // 2, PART, D), bf16)
        keep0, send0 = run_add(add_cores_kernel, section, keep0, got0, [half] * 2, "add_cores")
        keep0, send0, sent_grads, own_grads, own_rows = lax.optimization_barrier(
            (keep0, send0, sent_grads, own_grads, own_rows)
        )
        got0 = lax.ppermute(send0, "section", SWAP)
        layer_out = assemble(own_rows, got_rows, bf16)
        got0, layer_out, sums1, sent_grads, own_grads = lax.optimization_barrier(
            (got0, layer_out, sums1, sent_grads, own_grads)
        )
        one = jax.ShapeDtypeStruct((PART, D), bf16)
        blocks = run_add(
            add_sections_kernel, chip, keep0, got0, [one] * (BLOCKS // 2), "add_sections"
        )
        parts = [blocks[0]] + [exchange(blocks[d], d) for d in range(1, len(blocks))]
    else:
        packed0 = jnp.stack([keep0, send0], axis=1).reshape(GRADS.shape)
        parts = [lax.psum_scatter(split_shards(packed0, shards), SHARDED, scatter_dimension=0)]
        layer_out = assemble(own_rows, got_rows, bf16)
    got_grads = lax.ppermute(sent_grads, "section", SWAP)
    parts, sums1 = lax.optimization_barrier((parts, sums1))
    own_sums, sent_sums = run_parts(section, sums1, parts)
    got_sums = lax.ppermute(sent_sums, "section", SWAP)
    own_grads, own_sums = lax.optimization_barrier((own_grads, own_sums))
    input_out = assemble(own_grads, got_grads, f32)
    got_sums, input_out = lax.optimization_barrier((got_sums, input_out))
    finals = run_final(index, own_sums, got_sums, shards)
    return (
        layer_out.transpose(0, 2, 1, 3)[None],
        input_out.transpose(0, 2, 1, 3)[None],
        *[array[None] for array in finals],
    )


def solution(mesh):
    shape = (mesh.shape["section"], mesh.shape["fsdp"] // 2, 2)
    mesh = jax.sharding.Mesh(mesh.devices.reshape(shape), ("section", *SHARDED))
    in_specs = (
        P(None, SHARDED, None, None),
        P(None, SHARDED),
        P("section", None, SHARDED),
        P("section", None, SHARDED),
        P("section", SHARDED, None),
        P("section", SHARDED, None),
        P("section", SHARDED, None),
        P("section", SHARDED),
        P("section", SHARDED, None),
        P("section", None, None),
        P(None, SHARDED, None, None),
    )
    out_specs = (
        P("section", None, SHARDED, None, None),
        P("section", None, SHARDED, None, None),
        P("section", None, SHARDED),
        P("section", None, SHARDED),
        P("section", SHARDED, None),
        P("section", SHARDED, None),
        P("section", SHARDED, None),
        P("section", SHARDED),
        P("section", SHARDED, None),
        P("section", None, None),
    )
    return jax.shard_map(
        on_device, mesh=mesh, in_specs=in_specs, out_specs=out_specs, check_vma=False
    )
```
